512 devices in a mesh: gy: 16 (over z_hi, x, core), gx: 32 (over y, z_lo).
Axes of the slice: x: 4, y: 4, z: 16 (z_hi: 2, z_lo: 8; z = z_hi * 8 + z_lo), core: 2. Of those that a mesh axis runs over, the one named last changes fastest.
Arguments:
- heat_anomaly: float32 [75, 128, 4096], P(None, 'gy', 'gx'), may hold values from -6 to 6
- saltiness_anomaly: float32 [75, 128, 4096], P(None, 'gy', 'gx'), may hold values from -6 to 6
- eastward_transit_number: float32 [75, 128, 4096], P(None, 'gy', 'gx'), may hold values from -1.5 to 1.5
- poleward_transit_number: float32 [75, 128, 4096], P(None, 'gy', 'gx'), may hold values from -1.5 to 1.5
- rising_transit_number: float32 [75, 128, 4096], P(None, 'gy', 'gx'), may hold values from -1.5 to 1.5
- stacked_mixing_number: float32 [75, 128, 4096], P(None, 'gy', 'gx'), may hold values from 0.05 to 5
- neutral_mixing_number: float32 [128, 4096], P('gy', 'gx'), may hold values from 0.02 to 0.2
- ocean_strata_total: int32 [128, 4096], P('gy', 'gx'), may hold values from 0 to 75, as said below
Outputs:
- revised_heat_anomaly: float32 [75, 128, 4096], P(None, 'gy', 'gx')
- revised_saltiness: float32 [75, 128, 4096], P(None, 'gy', 'gx')
The draws below stay inside these ranges and needn't reach their ends.
Inputs may be any that keep to these rules, and one draw needn't show every extreme that they name: Levels k >= ocean_strata_total of a column are land; the southernmost row is land.
All inputs are finite; a program needn't handle non-finite values.
Results may differ from the reference program's by a relative error of at most 0.00002.
Values sent between devices are 32-bit elements; how exact they have to be, the bound alone decides.
No kernel may reach another device: no remote copies, remote signals or barrier semaphores. Data moves between devices by JAX's collectives and lax.ppermute only.
A program may use at most 64 MiB of HBM per device.

```python
import math
import jax
import jax.numpy as jnp
from jax import lax

STRATA_TOTAL = 75
CY = 8
CX = 128
LATITUDE_SPAN = 128
LONGITUDE_SPAN = 4096


def draw_ocean_strata_total(key, part):
    key = jax.random.fold_in(key, 11)
    tile_key, coast_key, depth_key = jax.random.split(key, 3)
    tile_open = jax.random.randint(tile_key, (LATITUDE_SPAN // CY, LONGITUDE_SPAN // CX), 0, 4)
    coast_draw = jax.random.randint(coast_key, (LATITUDE_SPAN, LONGITUDE_SPAN), 0, 6)
    depths_drawn = jax.random.randint(depth_key, (LATITUDE_SPAN, LONGITUDE_SPAN), 1, STRATA_TOTAL + 1)
    open_cells = jnp.repeat(jnp.repeat(tile_open, CY, axis=0), CX, axis=1)
    levels_out = jnp.where((open_cells > 0) & (coast_draw > 0), depths_drawn, 0)
    levels_out = levels_out.at[0, :].set(0)
    levels_out = levels_out.at[LATITUDE_SPAN // 2, LONGITUDE_SPAN // 2].set(STRATA_TOTAL)
    return levels_out.astype(jnp.int32)


def level_of(own_key, extent, cuts, smallest, largest):
    factor_of = 1.0
    for dim, shards_of in cuts:
        draws = jax.random.uniform(jax.random.fold_in(jax.random.fold_in(own_key, 6), dim), (shards_of,), jnp.float32, smallest / len(cuts), largest / len(cuts))
        factor_of = factor_of * jnp.repeat(jnp.exp(draws), extent[dim] // shards_of).reshape((-1,) + (1,) * (len(extent) - 1 - dim))
    return factor_of


def scatter_about(key, dims, deviation, most, cuts=(), kind=jnp.bfloat16):
    loudness = level_of(key, dims, cuts, -0.22, 0.18) if cuts else 1.0
    entries = jax.random.normal(key, dims, jnp.float32) * deviation * loudness
    return jnp.minimum(jnp.maximum(entries, -most), most).astype(kind)


def setup_inputs(seed: int = 0) -> dict:
    arg_keys = jax.random.split(jax.random.key(seed), 9)
    heat_anomaly = scatter_about(arg_keys[0], (STRATA_TOTAL, LATITUDE_SPAN, LONGITUDE_SPAN), 1.0, 6.0, ((1, 16), (2, 32)), jnp.float32)
    saltiness_anomaly = scatter_about(arg_keys[1], (STRATA_TOTAL, LATITUDE_SPAN, LONGITUDE_SPAN), 1.0, 6.0, ((1, 16), (2, 32)), jnp.float32)
    eastward_transit_number = scatter_about(arg_keys[2], (STRATA_TOTAL, LATITUDE_SPAN, LONGITUDE_SPAN), 0.1, 1.5, ((1, 16), (2, 32)), jnp.float32)
    poleward_transit_number = scatter_about(arg_keys[3], (STRATA_TOTAL, LATITUDE_SPAN, LONGITUDE_SPAN), 0.1, 1.5, ((1, 16), (2, 32)), jnp.float32)
    rising_transit_number = scatter_about(arg_keys[4], (STRATA_TOTAL, LATITUDE_SPAN, LONGITUDE_SPAN), 0.1, 1.5, ((1, 16), (2, 32)), jnp.float32)
    stacked_mixing_number = jnp.clip(jnp.exp(math.log(5.0) - 4.6051702 * jax.random.uniform(arg_keys[5], (STRATA_TOTAL, LATITUDE_SPAN, LONGITUDE_SPAN), jnp.float32) ** level_of(arg_keys[5], (STRATA_TOTAL, LATITUDE_SPAN, LONGITUDE_SPAN), ((1, 16), (2, 32)), -0.2, 0.2)), 0.05, 5.0)
    neutral_mixing_number = jnp.clip(jnp.exp(math.log(0.2) - 2.3025851 * jax.random.uniform(arg_keys[6], (LATITUDE_SPAN, LONGITUDE_SPAN), jnp.float32) ** level_of(arg_keys[6], (LATITUDE_SPAN, LONGITUDE_SPAN), ((0, 16), (1, 32)), -0.2, 0.2)), 0.02, 0.2)
    ocean_strata_total = draw_ocean_strata_total(jax.random.fold_in(arg_keys[8], 71), 0)
    return {"heat_anomaly": heat_anomaly, "saltiness_anomaly": saltiness_anomaly, "eastward_transit_number": eastward_transit_number, "poleward_transit_number": poleward_transit_number, "rising_transit_number": rising_transit_number, "stacked_mixing_number": stacked_mixing_number, "neutral_mixing_number": neutral_mixing_number, "ocean_strata_total": ocean_strata_total}


thermal_coef = 1.6550e-1
haline_coef = 7.6554e-1
thermal_curve = 5.9520e-2
haline_curve = 5.4914e-4
thermal_press = 1.4970e-4
haline_press = 1.1090e-5
cabbeling = 2.4341e-3
bottom_depth = 5800.0
slope_limit = 1.0
strat_offset = 0.1


def stratum_height_entry(level_count):
    level_index = jnp.arange(level_count, dtype=jnp.float32)
    return bottom_depth * ((level_index + 0.5) / level_count) ** 2


def density(temper, saline, strata_heights):
    return (-thermal_coef * (1.0 + 0.5 * thermal_curve * temper + thermal_press * strata_heights) * temper
            + haline_coef * (1.0 - 0.5 * haline_curve * saline - haline_press * strata_heights) * saline
            - cabbeling * temper * saline)


def column_diff(values_in, ocean_volume_flags):
    steps_up = (values_in[1:] - values_in[:-1]) * ocean_volume_flags[1:] * ocean_volume_flags[:-1]
    zeroed_stratum_sheet = jnp.zeros_like(values_in[:1])
    return 0.5 * (jnp.concatenate([zeroed_stratum_sheet, steps_up], 0) + jnp.concatenate([steps_up, zeroed_stratum_sheet], 0))


def volume_scalar_carry(temper, saline, ocean_share, diffus, strata_heights):
    level_count = temper.shape[0]
    level_index = jnp.arange(level_count, dtype=jnp.float32).reshape(level_count, 1, 1)
    ocean_volume_flags = jnp.where(level_index < ocean_share, 1.0, 0.0).astype(temper.dtype)
    dens = density(temper, saline, strata_heights.reshape(level_count, 1, 1))
    return (temper, saline, ocean_volume_flags, dens, column_diff(temper, ocean_volume_flags),
            column_diff(saline, ocean_volume_flags), column_diff(dens, ocean_volume_flags), diffus)


def face_flux(face_speed, left_cell, right_cell):
    face_wet = left_cell[2] * right_cell[2]
    face_diff = 0.5 * (left_cell[7] + right_cell[7])
    denominator = jnp.maximum(0.5 * (left_cell[6] + right_cell[6]), 0.0) + strat_offset
    slope_face = jnp.clip((right_cell[3] - left_cell[3]) / denominator, -slope_limit, slope_limit)
    forward = jnp.maximum(face_speed, 0.0)
    backward = jnp.minimum(face_speed, 0.0)
    flux_t = face_wet * (forward * left_cell[0] + backward * right_cell[0] - face_diff * (
        (right_cell[0] - left_cell[0]) - slope_face * 0.5 * (left_cell[4] + right_cell[4])))
    flux_s = face_wet * (forward * left_cell[1] + backward * right_cell[1] - face_diff * (
        (right_cell[1] - left_cell[1]) - slope_face * 0.5 * (left_cell[5] + right_cell[5])))
    return flux_t, flux_s


def tridiagonal_system_solver(rhs_t, rhs_s, vert_diff, ocean_volume_flags):
    coupling = vert_diff[1:] * ocean_volume_flags[1:] * ocean_volume_flags[:-1]
    zeroed_stratum_sheet = jnp.zeros_like(vert_diff[:1])
    coupling_above = jnp.concatenate([zeroed_stratum_sheet, coupling], 0)
    coupling_below = jnp.concatenate([coupling, zeroed_stratum_sheet], 0)
    center = 1.0 + coupling_above + coupling_below

    def forward(state_carry, level_items):
        prev_ratio, prev_t, prev_s = state_carry
        above_k, below_k, center_k, rhs_tk, rhs_sk = level_items
        pivot_value = center_k - above_k * prev_ratio
        next_ratio = below_k / pivot_value
        next_t = (rhs_tk + above_k * prev_t) / pivot_value
        next_s = (rhs_sk + above_k * prev_s) / pivot_value
        return (next_ratio, next_t, next_s), (next_ratio, next_t, next_s)

    start_plane = jnp.zeros_like(rhs_t[0])
    _, (ratios, part_t, part_s) = lax.scan(
        forward, (start_plane, start_plane, start_plane),
        (coupling_above, coupling_below, center, rhs_t, rhs_s))

    def backward(state_carry, level_items):
        below_t, below_s = state_carry
        ratio_k, part_tk, part_sk = level_items
        solved_t = part_tk + ratio_k * below_t
        solved_s = part_sk + ratio_k * below_s
        return (solved_t, solved_s), (solved_t, solved_s)

    _, (solved_t, solved_s) = lax.scan(backward, (start_plane, start_plane),
                                       (ratios, part_t, part_s), reverse=True)
    return solved_t, solved_s


def march_scalar_fields(heat_anomaly, saltiness_anomaly, eastern_heat_entry, eastern_saltiness, upper_heat_entry, upper_saltiness, rising_transit_number, stacked_mixing_number, ocean_volume_flags):
    joint_ocean_flags = ocean_volume_flags[1:] * ocean_volume_flags[:-1]
    backward_substitution_pass = jnp.maximum(rising_transit_number[1:], 0.0)
    forward_elimination = jnp.minimum(rising_transit_number[1:], 0.0)
    zeroed_stratum_sheet = jnp.zeros_like(heat_anomaly[:1])
    surface_heat_entry = jnp.concatenate([zeroed_stratum_sheet, joint_ocean_flags * (backward_substitution_pass * heat_anomaly[1:] + forward_elimination * heat_anomaly[:-1])], 0)
    top_s = jnp.concatenate([zeroed_stratum_sheet, joint_ocean_flags * (backward_substitution_pass * saltiness_anomaly[1:] + forward_elimination * saltiness_anomaly[:-1])], 0)
    seabed_heat_entry = jnp.concatenate([surface_heat_entry[1:], zeroed_stratum_sheet], 0)
    bottom_s = jnp.concatenate([top_s[1:], zeroed_stratum_sheet], 0)
    partial_heat_estimate = heat_anomaly - eastern_heat_entry - upper_heat_entry - (surface_heat_entry - seabed_heat_entry)
    provisional_saltiness = saltiness_anomaly - eastern_saltiness - upper_saltiness - (top_s - bottom_s)
    return tridiagonal_system_solver(partial_heat_estimate, provisional_saltiness, stacked_mixing_number, ocean_volume_flags)


def northward(member):
    return jnp.concatenate([member[..., 1:, :], member[..., -1:, ::-1]], -2)


def reference(heat_anomaly, saltiness_anomaly, eastward_transit_number, poleward_transit_number, rising_transit_number, stacked_mixing_number, neutral_mixing_number, ocean_strata_total):
    strata_heights = stratum_height_entry(heat_anomaly.shape[0])
    nearby_volumes = volume_scalar_carry(heat_anomaly, saltiness_anomaly, ocean_strata_total.astype(jnp.float32), neutral_mixing_number, strata_heights)
    east_cells = tuple(jnp.roll(member, -1, axis=-1) for member in nearby_volumes)
    north_cells = tuple(northward(member) for member in nearby_volumes)
    north_speed = jnp.concatenate(
        [poleward_transit_number[:, :-1], 0.5 * (poleward_transit_number[:, -1:] - poleward_transit_number[:, -1:, ::-1])], 1)
    heat_transport_right, flux_east_s = face_flux(eastward_transit_number, nearby_volumes, east_cells)
    heat_transport_upper, flux_north_s = face_flux(north_speed, nearby_volumes, north_cells)
    blank_latitude_line = jnp.zeros_like(heat_transport_upper[:, :1])
    eastern_heat_entry = heat_transport_right - jnp.roll(heat_transport_right, 1, axis=2)
    eastern_saltiness = flux_east_s - jnp.roll(flux_east_s, 1, axis=2)
    upper_heat_entry = heat_transport_upper - jnp.concatenate([blank_latitude_line, heat_transport_upper[:, :-1]], 1)
    upper_saltiness = flux_north_s - jnp.concatenate([blank_latitude_line, flux_north_s[:, :-1]], 1)
    return march_scalar_fields(heat_anomaly, saltiness_anomaly, eastern_heat_entry, eastern_saltiness, upper_heat_entry, upper_saltiness,
                   rising_transit_number, stacked_mixing_number, nearby_volumes[2])
```

```python
import functools

import jax
import jax.numpy as jnp
from jax import lax
from jax.experimental import pallas as pl
from jax.experimental.pallas import tpu as pltpu
from jax.sharding import PartitionSpec as P

thermal_coef = 0.1655
haline_coef = 0.76554
thermal_curve = 0.05952
haline_curve = 0.00054914
thermal_press = 0.0001497
haline_press = 1.109e-05
cabbeling = 0.0024341
bottom_depth = 5800.0
slope_limit = 1.0
strat_offset = 0.1

ROWS = 8
LANES = 128
GRID_AXES = ("gy", "gx")


def padded(levels):
    return -(-(levels + 2) // 8) * 8


def density(temper, saline, strata_height):
    heat_slope = -thermal_coef * (1.0 + thermal_press * strata_height)
    salt_slope = haline_coef * (1.0 - haline_press * strata_height)
    return (
        heat_slope - (0.5 * thermal_coef * thermal_curve) * temper - cabbeling * saline
    ) * temper + (salt_slope - (0.5 * haline_coef * haline_curve) * saline) * saline


def face_flux(speed, half_diffus, wet, left, right):
    denominator = jnp.maximum(0.25 * (left[5] + right[5]), 0.0) + strat_offset
    slope = jnp.clip((right[2] - left[2]) / denominator, -slope_limit, slope_limit)
    quarter = 0.25 * slope
    forward = speed > 0.0

    def one(i):
        carried = speed * jnp.where(forward, left[i], right[i])
        mixed = half_diffus * (right[i] - left[i] - quarter * (left[3 + i] + right[3 + i]))
        return jnp.where(wet, carried - mixed, 0.0)

    return one(0), one(1)


def pack_kernel(levels, t_ref, s_ref, u_ref, v_ref, diff_ref, depth_ref, a_ref, b_ref, xa_ref, xb_ref):
    block = padded(levels)
    gy, gx = lax.axis_index("gy"), lax.axis_index("gx")
    y_even, x_even = gy % 2 == 0, gx % 2 == 0
    is_top = gy == lax.axis_size("gy") - 1
    lane = lax.broadcasted_iota(jnp.int32, (block, LANES), 1)
    source = jnp.where(is_top, LANES - 1 - lane, lane)
    depth = depth_ref[...].astype(jnp.float32)
    diff = diff_ref[...]
    zero = jnp.zeros((block - levels - 2, LANES), jnp.float32)

    def rows(ref, r):
        return ref[pl.ds(r, levels, stride=ROWS), :]

    def part(ref, r, first):
        tail = [diff[r : r + 1], depth[r : r + 1], zero] if first else [jnp.zeros((block - levels, LANES), jnp.float32)]
        return jnp.concatenate([rows(ref, r)] + tail, 0)

    top = [part(t_ref, 7, True), part(s_ref, 7, False), part(v_ref, 7, False)]
    low = [part(t_ref, 0, True), part(s_ref, 0, False), jnp.zeros((block, LANES), jnp.float32)]
    for i in range(3):
        a_ref[i * block : (i + 1) * block] = jnp.where(y_even, top[i], low[i])
        b_ref[i * block : (i + 1) * block] = jnp.take_along_axis(
            jnp.where(y_even, low[i], top[i]), source, axis=1, mode="promise_in_bounds"
        )

    one_lane = lax.broadcasted_iota(jnp.int32, (ROWS, LANES), 1)

    def columns(ref, c, first):
        out = jnp.zeros((ROWS, LANES), jnp.float32)
        for k in range(levels):
            moved = pltpu.roll(ref[k * ROWS : (k + 1) * ROWS], (k - c) % LANES, 1)
            out = jnp.where(one_lane == k, moved, out)
        if first:
            out = jnp.where(one_lane == levels, pltpu.roll(diff, (levels - c) % LANES, 1), out)
            out = jnp.where(one_lane == levels + 1, pltpu.roll(depth, (levels + 1 - c) % LANES, 1), out)
        return out

    east = [columns(t_ref, 127, True), columns(s_ref, 127, False), columns(u_ref, 127, False)]
    west = [columns(t_ref, 0, True), columns(s_ref, 0, False), jnp.zeros((ROWS, LANES), jnp.float32)]
    for i in range(3):
        xa_ref[i * ROWS : (i + 1) * ROWS] = jnp.where(x_even, east[i], west[i])
        xb_ref[i * ROWS : (i + 1) * ROWS] = jnp.where(x_even, west[i], east[i])


def inner_kernel(
    levels, group, t_ref, s_ref, u_ref, v_ref, w_ref, kap_ref, diff_ref, depth_ref,
    star_t_ref, star_s_ref, inv_ref, low_ref, ratio_ref, own_ref,
):
    block = padded(levels)
    depth = depth_ref[...]
    diff = diff_ref[...]
    lane = lax.broadcasted_iota(jnp.int32, (ROWS, LANES), 1)
    row = lax.broadcasted_iota(jnp.int32, (ROWS, LANES), 0)

    def east(x):
        return pltpu.roll(x, LANES - 1, 1)

    def west(x):
        return pltpu.roll(x, 1, 1)

    def north(x):
        return pltpu.roll(x, ROWS - 1, 0)

    def south(x):
        return pltpu.roll(x, 1, 0)

    depth_x = jnp.where(lane == LANES - 1, 0, jnp.minimum(depth, east(depth)))
    depth_y = jnp.where(row == ROWS - 1, 0, jnp.minimum(depth, north(depth)))
    diff_x = 0.5 * (diff + east(diff))
    diff_y = 0.5 * (diff + north(diff))

    def at(ref, k):
        return ref[k]

    def height(k):
        part = (k.astype(jnp.float32) + 0.5) / levels
        return bottom_depth * (part * part)

    def level(k, carry):
        t, s, dens, step_t, step_s, step_d, top_t, top_s = carry
        below = jnp.minimum(k + 1, levels - 1)
        open_below = k + 1 < depth
        t1, s1 = at(t_ref, below), at(s_ref, below)
        dens1 = density(t1, s1, height(below))
        next_t = jnp.where(open_below, t1 - t, 0.0)
        next_s = jnp.where(open_below, s1 - s, 0.0)
        next_d = jnp.where(open_below, dens1 - dens, 0.0)
        w1 = at(w_ref, below)
        up = w1 > 0.0
        low_t = jnp.where(open_below, w1 * jnp.where(up, t1, t), 0.0)
        low_s = jnp.where(open_below, w1 * jnp.where(up, s1, s), 0.0)
        here = (t, s, dens, step_t + next_t, step_s + next_s, step_d + next_d)
        fx_t, fx_s = face_flux(at(u_ref, k), diff_x, k < depth_x, here, tuple(map(east, here)))
        fy_t, fy_s = face_flux(at(v_ref, k), diff_y, k < depth_y, here, tuple(map(north, here)))
        star_t_ref[k] = t - (fx_t - west(fx_t)) - (fy_t - south(fy_t)) - (top_t - low_t)
        star_s_ref[k] = s - (fx_s - west(fx_s)) - (fy_s - south(fy_s)) - (top_s - low_s)
        return t1, s1, dens1, next_t, next_s, next_d, low_t, low_s

    zero = jnp.zeros((ROWS, LANES), jnp.float32)
    t0, s0 = t_ref[0], s_ref[0]
    first = (t0, s0, density(t0, s0, bottom_depth * (0.5 / levels) ** 2), zero, zero, zero, zero, zero)

    def some(i, carry):
        for j in range(group):
            carry = level(i * group + j, carry)
        return carry

    lax.fori_loop(0, levels // group, some, first)

    middle = levels // 2

    def coupling(k):
        return jnp.where(k < depth, kap_ref[k], 0.0)

    def eliminate(j, carry):
        above, ratio, below, ratio_up = carry
        k = j
        under = coupling(k + 1)
        inv = 1.0 / (1.0 + above + under - above * ratio)
        inv_ref[k] = inv
        low_ref[k] = above * inv
        ratio = under * inv
        ratio_ref[k] = ratio
        k = levels - 1 - j
        over = coupling(k)
        inv = 1.0 / (1.0 + over + below - below * ratio_up)
        inv_ref[k] = inv
        low_ref[k] = below * inv
        ratio_up = over * inv
        ratio_ref[k] = ratio_up
        return under, ratio, over, ratio_up

    above, ratio, below, ratio_up = lax.fori_loop(0, middle, eliminate, (zero, zero, zero, zero))
    inv = 1.0 / (1.0 + above + below - above * ratio - below * ratio_up)
    inv_ref[middle] = inv
    low_ref[middle] = above * inv
    ratio_ref[middle] = below * inv

    gy = lax.axis_index("gy")
    y_even = gy % 2 == 0
    tail = jnp.zeros((block - levels, LANES), jnp.float32)
    extra = jnp.zeros((block - levels - 2, LANES), jnp.float32)
    depth_f = depth.astype(jnp.float32)
    for i, ref in enumerate((t_ref, s_ref, v_ref)):
        flat = ref.reshape(levels * ROWS, LANES)
        for place, keep_top in ((0, y_even), (1, jnp.logical_not(y_even))):
            top = flat[pl.ds(ROWS - 1, levels, stride=ROWS), :]
            low = flat[pl.ds(0, levels, stride=ROWS), :]
            end = tail
            if i == 0:
                end = jnp.concatenate(
                    [
                        jnp.where(keep_top, diff[ROWS - 1 :], diff[:1]),
                        jnp.where(keep_top, depth_f[ROWS - 1 :], depth_f[:1]),
                        extra,
                    ],
                    0,
                )
            own_ref[place, i] = jnp.concatenate([jnp.where(keep_top, top, low), end], 0)


def column_sums(x, open_here, axis):
    size = x.shape[axis]
    step = jnp.where(open_here, x - pltpu.roll(x, 1, axis), 0.0)
    return step + pltpu.roll(step, size - 1, axis)


def side(temper, saline, depth, index, heights, axis):
    dens = density(temper, saline, heights)
    open_here = jnp.logical_and(index >= 1, index < depth)
    return (
        temper,
        saline,
        dens,
        column_sums(temper, open_here, axis),
        column_sums(saline, open_here, axis),
        column_sums(dens, open_here, axis),
    )


def edge_flux(levels, axis, index, own, got, own_left, fold):
    part = (index.astype(jnp.float32) + 0.5) / levels
    heights = bottom_depth * (part * part)
    left = [jnp.where(own_left, o, g) for o, g in zip(own, got)]
    right = [jnp.where(own_left, g, o) for o, g in zip(own, got)]
    speed = left[2]
    if fold is not None:
        speed = jnp.where(fold, 0.5 * (own[2] - got[2]), speed)
    wet = index.astype(jnp.float32) < jnp.minimum(left[4], right[4])
    level = index.astype(jnp.float32)
    return face_flux(
        speed,
        0.5 * (left[3] + right[3]),
        wet,
        side(left[0], left[1], left[4], level, heights, axis),
        side(right[0], right[1], right[4], level, heights, axis),
    )


def final_kernel(
    levels, got_a, got_b, got_xa, got_xb, own_ref, own_xa, own_xb,
    star_t_ref, star_s_ref, inv_ref, low_ref, ratio_ref,
    out_t_ref, out_s_ref, north_ref, south_ref,
):
    block = padded(levels)
    gy, gx = lax.axis_index("gy"), lax.axis_index("gx")
    y_even, x_even = gy % 2 == 0, gx % 2 == 0
    y_odd, x_odd = jnp.logical_not(y_even), jnp.logical_not(x_even)
    is_top = gy == lax.axis_size("gy") - 1

    index = lax.broadcasted_iota(jnp.int32, (block, LANES), 0)

    def rows(ref):
        t, s, q = ref[0], ref[1], ref[2]
        return t, s, q, t[levels : levels + 1], t[levels + 1 : levels + 2]

    flux_a = edge_flux(levels, 0, index, rows(own_ref.at[0]), rows(got_a), y_even, None)
    flux_b = edge_flux(levels, 0, index, rows(own_ref.at[1]), rows(got_b), y_odd, is_top)
    for i in range(2):
        north_ref[i] = -jnp.where(y_even, flux_a[i], flux_b[i])
        south_ref[i] = jnp.where(y_even, flux_b[i], flux_a[i])

    lane = lax.broadcasted_iota(jnp.int32, (ROWS, LANES), 1)
    row = lax.broadcasted_iota(jnp.int32, (ROWS, LANES), 0)

    def cols(ref):
        t, s, q = ref[0], ref[1], ref[2]
        return t, s, q, t[:, levels : levels + 1], t[:, levels + 1 : levels + 2]

    flux_xa = edge_flux(levels, 1, lane, cols(own_xa), cols(got_xa), x_even, None)
    flux_xb = edge_flux(levels, 1, lane, cols(own_xb), cols(got_xb), x_odd, None)
    east = [-jnp.where(x_even, flux_xa[i], flux_xb[i]) for i in range(2)]
    west = [jnp.where(x_even, flux_xb[i], flux_xa[i]) for i in range(2)]
    last_lane, first_lane = lane == LANES - 1, lane == 0
    last_row, first_row = row == ROWS - 1, row == 0

    def right_side(i, k):
        ref = (star_t_ref, star_s_ref)[i]
        x_part = jnp.where(
            last_lane,
            pltpu.roll(east[i], (LANES - 1 - k) % LANES, 1),
            jnp.where(first_lane, pltpu.roll(west[i], (-k) % LANES, 1), 0.0),
        )
        y_part = jnp.where(
            last_row,
            north_ref[i, k : k + 1, :],
            jnp.where(first_row, south_ref[i, k : k + 1, :], 0.0),
        )
        return (ref[k] + (x_part + y_part)) * inv_ref[k]

    outs = (out_t_ref, out_s_ref)
    middle = levels // 2
    zero = jnp.zeros((ROWS, LANES), jnp.float32)
    upper, lower = [zero, zero], [zero, zero]
    for j in range(middle):
        for i in range(2):
            upper[i] = right_side(i, j) + low_ref[j] * upper[i]
            outs[i][j] = upper[i]
            k = levels - 1 - j
            lower[i] = right_side(i, k) + low_ref[k] * lower[i]
            outs[i][k] = lower[i]
    for i in range(2):
        solved = right_side(i, middle) + low_ref[middle] * upper[i] + ratio_ref[middle] * lower[i]
        outs[i][middle] = solved
        upper[i] = lower[i] = solved
    for j in range(1, middle + 1):
        for i in range(2):
            k = middle - j
            upper[i] = outs[i][k] + ratio_ref[k] * upper[i]
            outs[i][k] = upper[i]
            k = middle + j
            lower[i] = outs[i][k] + ratio_ref[k] * lower[i]
            outs[i][k] = lower[i]


def call(kernel, outs, n_in, scratch=(), flops=0, name=None):
    return pl.pallas_call(
        kernel,
        out_shape=[jax.ShapeDtypeStruct(s, jnp.float32) for s in outs],
        in_specs=[pl.BlockSpec(memory_space=pltpu.VMEM)] * n_in,
        out_specs=[pl.BlockSpec(memory_space=pltpu.VMEM)] * len(outs),
        scratch_shapes=[pltpu.VMEM(s, jnp.float32) for s in scratch],
        compiler_params=pltpu.CompilerParams(vmem_limit_bytes=24 * 1024 * 1024),
        cost_estimate=pl.CostEstimate(flops=flops, bytes_accessed=4 * 1024 * 1024, transcendentals=0),
        name=name,
    )


def local(pairs, heat, salt, u, v, w, kap, diff, depth):
    levels, rows, lanes = heat.shape
    block = padded(levels)

    def flat(x):
        return x.reshape(levels * rows, lanes)

    pack_a, pack_b, pack_xa, pack_xb = call(
        functools.partial(pack_kernel, levels),
        [(3 * block, lanes)] * 2 + [(3 * rows, lanes)] * 2, 6, name="pack",
    )(flat(heat), flat(salt), flat(u), flat(v), diff, depth)
    got_b = lax.ppermute(pack_b, GRID_AXES, pairs["b"])
    got_xb = lax.ppermute(pack_xb, "gx", pairs["xb"])
    got_xa = lax.ppermute(pack_xa, "gx", pairs["xa"])
    got_a = lax.ppermute(pack_a, GRID_AXES, pairs["a"])
    cube = (levels, rows, lanes)
    group = next(g for g in (5, 3, 2, 1) if levels % g == 0)
    star_t, star_s, inv, low, ratio, own = call(
        functools.partial(inner_kernel, levels, group),
        [cube] * 5 + [(2, 3, block, lanes)], 8, flops=40_000_000, name="inner",
    )(heat, salt, u, v, w, kap, diff, depth)
    three = (3, rows, lanes)
    return call(
        functools.partial(final_kernel, levels),
        [cube] * 2, 12, scratch=[(2, block, lanes)] * 2, name="final",
    )(
        got_a.reshape(3, block, lanes), got_b.reshape(3, block, lanes),
        got_xa.reshape(three), got_xb.reshape(three),
        own, pack_xa.reshape(three), pack_xb.reshape(three),
        star_t, star_s, inv, low, ratio,
    )


def solution(mesh):
    ny, nx = mesh.shape["gy"], mesh.shape["gx"]

    def at(y, x):
        return y * nx + x

    pairs = {
        "a": [(at(y, x), at(y ^ 1, x)) for y in range(ny) for x in range(nx)],
        "b": [(at(y, x), at(((y + 1) ^ 1) - 1, x)) for y in range(1, ny - 1) for x in range(nx)]
        + [(at(ny - 1, x), at(ny - 1, nx - 1 - x)) for x in range(nx)],
        "xa": [(x, x ^ 1) for x in range(nx)],
        "xb": [(x, (((x + 1) ^ 1) - 1) % nx) for x in range(nx)],
    }
    cube = P(None, "gy", "gx")
    sheet = P("gy", "gx")
    return jax.shard_map(
        functools.partial(local, pairs),
        mesh=mesh,
        in_specs=(cube,) * 6 + (sheet, sheet),
        out_specs=(cube, cube),
        check_vma=False,
    )
```

```python
import functools

import jax
import jax.numpy as jnp
from jax import lax
from jax.experimental import pallas as pl
from jax.experimental.pallas import tpu as pltpu
from jax.sharding import PartitionSpec as P

thermal_coef = 0.1655
haline_coef = 0.76554
thermal_curve = 0.05952
haline_curve = 0.00054914
thermal_press = 0.0001497
haline_press = 1.109e-05
cabbeling = 0.0024341
bottom_depth = 5800.0
slope_limit = 1.0
strat_offset = 0.1

ROWS = 8
LANES = 128
GRID_AXES = ("gy", "gx")


def padded(levels):
    return -(-(levels + 2) // 8) * 8


def density(temper, saline, strata_height):
    heat_slope = -thermal_coef * (1.0 + thermal_press * strata_height)
    salt_slope = haline_coef * (1.0 - haline_press * strata_height)
    return (
        heat_slope - (0.5 * thermal_coef * thermal_curve) * temper - cabbeling * saline
    ) * temper + (salt_slope - (0.5 * haline_coef * haline_curve) * saline) * saline


def face_flux(speed, half_diffus, wet, left, right):
    denominator = jnp.maximum(0.25 * (left[5] + right[5]), 0.0) + strat_offset
    slope = jnp.clip((right[2] - left[2]) / denominator, -slope_limit, slope_limit)
    quarter = 0.25 * slope
    forward = speed > 0.0

    def one(i):
        carried = speed * jnp.where(forward, left[i], right[i])
        mixed = half_diffus * (right[i] - left[i] - quarter * (left[3 + i] + right[3 + i]))
        return jnp.where(wet, carried - mixed, 0.0)

    return one(0), one(1)


def fetch(sources, targets, sems):
    copies = [pltpu.make_async_copy(a, b, sems.at[i]) for i, (a, b) in enumerate(zip(sources, targets))]
    for copy in copies:
        copy.start()
    return copies


def pack_kernel(
    levels, t_hbm, s_hbm, v_hbm, u_hbm, diff_hbm, depth_hbm, a_ref, b_ref, xb_ref, xa_ref,
    t_ref, s_ref, v_ref, u_ref, diff_ref, depth_ref, sems,
):
    copies = fetch(
        (t_hbm, s_hbm, v_hbm, u_hbm, diff_hbm, depth_hbm),
        (t_ref, s_ref, v_ref, u_ref, diff_ref, depth_ref),
        sems,
    )
    block = padded(levels)
    gy, gx = lax.axis_index("gy"), lax.axis_index("gx")
    y_even, x_even = gy % 2 == 0, gx % 2 == 0
    is_top = gy == lax.axis_size("gy") - 1
    lane = lax.broadcasted_iota(jnp.int32, (block, LANES), 1)
    source = jnp.where(is_top, LANES - 1 - lane, lane)
    one_lane = lax.broadcasted_iota(jnp.int32, (ROWS, LANES), 1)
    copies[4].wait()
    copies[5].wait()
    depth = depth_ref[...].astype(jnp.float32)
    diff = diff_ref[...]
    zero = jnp.zeros((block - levels - 2, LANES), jnp.float32)
    tail = jnp.zeros((block - levels, LANES), jnp.float32)

    def row_part(ref, i):
        top = ref[pl.ds(ROWS - 1, levels, stride=ROWS), :]
        low = ref[pl.ds(0, levels, stride=ROWS), :]
        end = tail
        if i == 0:
            end = jnp.concatenate(
                [
                    jnp.where(y_even, diff[:1], diff[ROWS - 1 :]),
                    jnp.where(y_even, depth[:1], depth[ROWS - 1 :]),
                    zero,
                ],
                0,
            )
        chosen = jnp.concatenate([jnp.where(y_even, low, top), end], 0)
        if i == 0:
            end = jnp.concatenate(
                [
                    jnp.where(y_even, diff[ROWS - 1 :], diff[:1]),
                    jnp.where(y_even, depth[ROWS - 1 :], depth[:1]),
                    zero,
                ],
                0,
            )
        a_ref[i * block : (i + 1) * block] = jnp.concatenate([jnp.where(y_even, top, low), end], 0)
        b_ref[i * block : (i + 1) * block] = jnp.take_along_axis(
            chosen, source, axis=1, mode="promise_in_bounds"
        )

    def columns(ref, c, first):
        out = jnp.zeros((ROWS, LANES), jnp.float32)
        for k in range(levels):
            moved = pltpu.roll(ref[k * ROWS : (k + 1) * ROWS], (k - c) % LANES, 1)
            out = jnp.where(one_lane == k, moved, out)
        if first:
            out = jnp.where(one_lane == levels, pltpu.roll(diff, (levels - c) % LANES, 1), out)
            out = jnp.where(one_lane == levels + 1, pltpu.roll(depth, (levels + 1 - c) % LANES, 1), out)
        return out

    def column_part(ref, i):
        east = columns(ref, LANES - 1, i == 0)
        west = columns(ref, 0, i == 0) if i < 2 else jnp.zeros((ROWS, LANES), jnp.float32)
        xa_ref[i * ROWS : (i + 1) * ROWS] = jnp.where(x_even, east, west)
        xb_ref[i * ROWS : (i + 1) * ROWS] = jnp.where(x_even, west, east)

    for i, ref in enumerate((t_ref, s_ref)):
        copies[i].wait()
        row_part(ref, i)
        column_part(ref, i)
    copies[2].wait()
    row_part(v_ref, 2)
    copies[3].wait()
    column_part(u_ref, 2)


def inner_kernel(
    levels, group, t_hbm, s_hbm, u_hbm, v_hbm, w_hbm, kap_hbm, diff_hbm, depth_hbm,
    star_t_ref, star_s_ref, inv_ref, low_ref, ratio_ref, own_a_ref, own_b_ref,
    t_ref, s_ref, u_ref, v_ref, w_ref, kap_ref, diff_ref, depth_ref, sems,
):
    copies = fetch(
        (t_hbm, s_hbm, u_hbm, v_hbm, w_hbm, kap_hbm, diff_hbm, depth_hbm),
        (t_ref, s_ref, u_ref, v_ref, w_ref, kap_ref, diff_ref, depth_ref),
        sems,
    )
    for copy in copies:
        copy.wait()
    block = padded(levels)
    depth = depth_ref[...]
    diff = diff_ref[...]
    lane = lax.broadcasted_iota(jnp.int32, (ROWS, LANES), 1)
    row = lax.broadcasted_iota(jnp.int32, (ROWS, LANES), 0)

    def east(x):
        return pltpu.roll(x, LANES - 1, 1)

    def west(x):
        return pltpu.roll(x, 1, 1)

    def north(x):
        return pltpu.roll(x, ROWS - 1, 0)

    def south(x):
        return pltpu.roll(x, 1, 0)

    depth_x = jnp.where(lane == LANES - 1, 0, jnp.minimum(depth, east(depth)))
    depth_y = jnp.where(row == ROWS - 1, 0, jnp.minimum(depth, north(depth)))
    diff_x = 0.5 * (diff + east(diff))
    diff_y = 0.5 * (diff + north(diff))

    def at(ref, k):
        return ref[k]

    def height(k):
        part = (k.astype(jnp.float32) + 0.5) / levels
        return bottom_depth * (part * part)

    def level(k, carry):
        t, s, dens, step_t, step_s, step_d, top_t, top_s = carry
        below = jnp.minimum(k + 1, levels - 1)
        open_below = k + 1 < depth
        t1, s1 = at(t_ref, below), at(s_ref, below)
        dens1 = density(t1, s1, height(below))
        next_t = jnp.where(open_below, t1 - t, 0.0)
        next_s = jnp.where(open_below, s1 - s, 0.0)
        next_d = jnp.where(open_below, dens1 - dens, 0.0)
        w1 = at(w_ref, below)
        up = w1 > 0.0
        low_t = jnp.where(open_below, w1 * jnp.where(up, t1, t), 0.0)
        low_s = jnp.where(open_below, w1 * jnp.where(up, s1, s), 0.0)
        here = (t, s, dens, step_t + next_t, step_s + next_s, step_d + next_d)
        fx_t, fx_s = face_flux(at(u_ref, k), diff_x, k < depth_x, here, tuple(map(east, here)))
        fy_t, fy_s = face_flux(at(v_ref, k), diff_y, k < depth_y, here, tuple(map(north, here)))
        star_t_ref[k] = t - (fx_t - west(fx_t)) - (fy_t - south(fy_t)) - (top_t - low_t)
        star_s_ref[k] = s - (fx_s - west(fx_s)) - (fy_s - south(fy_s)) - (top_s - low_s)
        return t1, s1, dens1, next_t, next_s, next_d, low_t, low_s

    zero = jnp.zeros((ROWS, LANES), jnp.float32)
    t0, s0 = t_ref[0], s_ref[0]
    first = (t0, s0, density(t0, s0, bottom_depth * (0.5 / levels) ** 2), zero, zero, zero, zero, zero)

    def some(i, carry):
        for j in range(group):
            carry = level(i * group + j, carry)
        return carry

    lax.fori_loop(0, levels // group, some, first)

    middle = levels // 2

    def coupling(k):
        return jnp.where(k < depth, kap_ref[k], 0.0)

    def eliminate(j, carry):
        above, ratio, below, ratio_up = carry
        k = j
        under = coupling(k + 1)
        inv = 1.0 / (1.0 + above + under - above * ratio)
        inv_ref[k] = inv
        low_ref[k] = above * inv
        ratio = under * inv
        ratio_ref[k] = ratio
        k = levels - 1 - j
        over = coupling(k)
        inv = 1.0 / (1.0 + over + below - below * ratio_up)
        inv_ref[k] = inv
        low_ref[k] = below * inv
        ratio_up = over * inv
        ratio_ref[k] = ratio_up
        return under, ratio, over, ratio_up

    above, ratio, below, ratio_up = lax.fori_loop(0, middle, eliminate, (zero, zero, zero, zero))
    inv = 1.0 / (1.0 + above + below - above * ratio - below * ratio_up)
    inv_ref[middle] = inv
    low_ref[middle] = above * inv
    ratio_ref[middle] = below * inv

    gy = lax.axis_index("gy")
    y_even = gy % 2 == 0
    tail = jnp.zeros((block - levels, LANES), jnp.float32)
    extra = jnp.zeros((block - levels - 2, LANES), jnp.float32)
    depth_f = depth.astype(jnp.float32)
    for i, ref in enumerate((t_ref, s_ref, v_ref)):
        flat = ref.reshape(levels * ROWS, LANES)
        for own_ref, keep_top in ((own_a_ref, y_even), (own_b_ref, jnp.logical_not(y_even))):
            top = flat[pl.ds(ROWS - 1, levels, stride=ROWS), :]
            low = flat[pl.ds(0, levels, stride=ROWS), :]
            end = tail
            if i == 0:
                end = jnp.concatenate(
                    [
                        jnp.where(keep_top, diff[ROWS - 1 :], diff[:1]),
                        jnp.where(keep_top, depth_f[ROWS - 1 :], depth_f[:1]),
                        extra,
                    ],
                    0,
                )
            own_ref[i * block : (i + 1) * block] = jnp.concatenate([jnp.where(keep_top, top, low), end], 0)


def column_sums(x, open_here, axis):
    size = x.shape[axis]
    step = jnp.where(open_here, x - pltpu.roll(x, 1, axis), 0.0)
    return step + pltpu.roll(step, size - 1, axis)


def side(temper, saline, depth, index, heights, axis):
    dens = density(temper, saline, heights)
    open_here = jnp.logical_and(index >= 1, index < depth)
    return (
        temper,
        saline,
        dens,
        column_sums(temper, open_here, axis),
        column_sums(saline, open_here, axis),
        column_sums(dens, open_here, axis),
    )


def edge_flux(levels, axis, index, own, got, own_left, fold):
    part = (index.astype(jnp.float32) + 0.5) / levels
    heights = bottom_depth * (part * part)
    left = [jnp.where(own_left, o, g) for o, g in zip(own, got)]
    right = [jnp.where(own_left, g, o) for o, g in zip(own, got)]
    speed = left[2]
    if fold is not None:
        speed = jnp.where(fold, 0.5 * (own[2] - got[2]), speed)
    wet = index.astype(jnp.float32) < jnp.minimum(left[4], right[4])
    level = index.astype(jnp.float32)
    return face_flux(
        speed,
        0.5 * (left[3] + right[3]),
        wet,
        side(left[0], left[1], left[4], level, heights, axis),
        side(right[0], right[1], right[4], level, heights, axis),
    )


def final_kernel(
    levels, cut, got_a, got_b, got_xa, got_xb, got_relay, own_a, own_b, own_xa, own_xb,
    star_t_ref, star_s_ref, inv_ref, low_ref, ratio_ref,
    out_t_ref, out_s_ref, north_ref, south_ref,
):
    block = padded(levels)
    gy, gx = lax.axis_index("gy"), lax.axis_index("gx")
    y_even, x_even = gy % 2 == 0, gx % 2 == 0
    y_odd, x_odd = jnp.logical_not(y_even), jnp.logical_not(x_even)
    is_top = gy == lax.axis_size("gy") - 1

    index = lax.broadcasted_iota(jnp.int32, (block, LANES), 0)

    corner = jnp.logical_and(is_far_row(gy), is_far_column(gx, cut))

    def rows(ref):
        t, s, q = (ref[i * block : (i + 1) * block] for i in range(3))
        return t, s, q, t[levels : levels + 1], t[levels + 1 : levels + 2]

    flux_a = edge_flux(levels, 0, index, rows(own_a), rows(got_a), y_even, None)
    flux_b = edge_flux(levels, 0, index, rows(own_b), rows(got_b), y_odd, is_top)
    for i in range(2):
        north_ref[i] = -jnp.where(y_even, flux_a[i], flux_b[i])
        south_ref[i] = jnp.where(y_even, flux_b[i], flux_a[i])

    lane = lax.broadcasted_iota(jnp.int32, (ROWS, LANES), 1)
    row = lax.broadcasted_iota(jnp.int32, (ROWS, LANES), 0)

    def cols(ref, other=None):
        t, s, q = (
            ref[i * ROWS : (i + 1) * ROWS]
            if other is None
            else jnp.where(corner, other[i * ROWS : (i + 1) * ROWS], ref[i * ROWS : (i + 1) * ROWS])
            for i in range(3)
        )
        return t, s, q, t[:, levels : levels + 1], t[:, levels + 1 : levels + 2]

    flux_xa = edge_flux(levels, 1, lane, cols(own_xa), cols(got_xa), x_even, None)
    flux_xb = edge_flux(levels, 1, lane, cols(own_xb), cols(got_xb, got_relay), x_odd, None)
    east = [-jnp.where(x_even, flux_xa[i], flux_xb[i]) for i in range(2)]
    west = [jnp.where(x_even, flux_xb[i], flux_xa[i]) for i in range(2)]
    last_lane, first_lane = lane == LANES - 1, lane == 0
    last_row, first_row = row == ROWS - 1, row == 0

    def right_side(i, k):
        ref = (star_t_ref, star_s_ref)[i]
        x_part = jnp.where(
            last_lane,
            pltpu.roll(east[i], (LANES - 1 - k) % LANES, 1),
            jnp.where(first_lane, pltpu.roll(west[i], (-k) % LANES, 1), 0.0),
        )
        y_part = jnp.where(
            last_row,
            north_ref[i, k : k + 1, :],
            jnp.where(first_row, south_ref[i, k : k + 1, :], 0.0),
        )
        return (ref[k] + (x_part + y_part)) * inv_ref[k]

    outs = (out_t_ref, out_s_ref)
    middle = levels // 2
    zero = jnp.zeros((ROWS, LANES), jnp.float32)
    upper, lower = [zero, zero], [zero, zero]
    for j in range(middle):
        for i in range(2):
            upper[i] = right_side(i, j) + low_ref[j] * upper[i]
            outs[i][j] = upper[i]
            k = levels - 1 - j
            lower[i] = right_side(i, k) + low_ref[k] * lower[i]
            outs[i][k] = lower[i]
    for i in range(2):
        solved = right_side(i, middle) + low_ref[middle] * upper[i] + ratio_ref[middle] * lower[i]
        outs[i][middle] = solved
        upper[i] = lower[i] = solved
    for j in range(1, middle + 1):
        for i in range(2):
            k = middle - j
            upper[i] = outs[i][k] + ratio_ref[k] * upper[i]
            outs[i][k] = upper[i]
            k = middle + j
            lower[i] = outs[i][k] + ratio_ref[k] * lower[i]
            outs[i][k] = lower[i]


def call(kernel, outs, operands, memory, scratch=(), flops=0, name=None):
    return pl.pallas_call(
        kernel,
        out_shape=[jax.ShapeDtypeStruct(s, jnp.float32) for s in outs],
        in_specs=[pl.BlockSpec(memory_space=memory)] * len(operands),
        out_specs=[pl.BlockSpec(memory_space=pltpu.VMEM)] * len(outs),
        scratch_shapes=list(scratch),
        compiler_params=pltpu.CompilerParams(vmem_limit_bytes=24 * 1024 * 1024),
        cost_estimate=pl.CostEstimate(flops=flops, bytes_accessed=4 * 1024 * 1024, transcendentals=0),
        name=name,
    )(*operands)


def local(pairs, cut, heat, salt, u, v, w, kap, diff, depth):
    levels, rows, lanes = heat.shape
    block = padded(levels)
    cube, wide, thin = (levels, rows, lanes), (3 * block, lanes), (3 * rows, lanes)

    def flat(x):
        return x.reshape(levels * rows, lanes)

    def room(operands):
        return [pltpu.VMEM(x.shape, x.dtype) for x in operands] + [pltpu.SemaphoreType.DMA((len(operands),))]

    def moved(x, which):
        return lax.ppermute(x, GRID_AXES, pairs[which])

    operands = tuple(pltpu.with_memory_space_constraint(x, pltpu.HBM) for x in (flat(heat), flat(salt), flat(v), flat(u), diff, depth))
    pack_a, pack_b, pack_xb, pack_xa = call(
        functools.partial(pack_kernel, levels), [wide, wide, thin, thin], operands, pltpu.HBM, room(operands), name="pack"
    )
    got_a = moved(pack_a, "a")
    got_b = moved(pack_b, "b")
    relayed = moved(pack_xb, "relay")
    got_xb = moved(pack_xb, "xb")
    got_xa = moved(pack_xa, "xa")
    group = next(g for g in (5, 3, 2, 1) if levels % g == 0)
    operands = tuple(pltpu.with_memory_space_constraint(x, pltpu.HBM) for x in (heat, salt, u, v, w, kap, diff, depth))
    star_t, star_s, inv, low, ratio, own_a, own_b = call(
        functools.partial(inner_kernel, levels, group),
        [cube] * 5 + [wide, wide], operands, pltpu.HBM, room(operands), flops=40_000_000, name="inner",
    )
    relayed, star_t = lax.optimization_barrier((relayed, star_t))
    got_relay = moved(relayed, "hand_on")
    operands = (
        got_a, got_b, got_xa, got_xb, got_relay, own_a, own_b, pack_xa, pack_xb,
        star_t, star_s, inv, low, ratio,
    )
    return call(
        functools.partial(final_kernel, levels, cut),
        [cube] * 2, operands, pltpu.VMEM, [pltpu.VMEM((2, block, lanes), jnp.float32)] * 2, name="final",
    )


def is_far_row(y):
    ny = lax.axis_size("gy")
    return (y == ny // 2 - 1) | (y == ny // 2) | (y == ny - 1)


def is_far_column(x, cut):
    return (x % cut == 0) | (x % cut == cut - 1)


def solution(mesh):
    ny, nx = mesh.shape["gy"], mesh.shape["gx"]
    cut = nx // 4
    far_rows = (ny // 2 - 1, ny // 2, ny - 1)
    far_columns = [x for x in range(nx) if x % cut in (0, cut - 1)]

    def at(y, x):
        return y * nx + x

    def beside(x):
        return (((x + 1) ^ 1) - 1) % nx

    second = [(y, ((y + 1) ^ 1) - 1, x, x) for y in range(1, ny - 1) for x in range(nx)]
    second += [(ny - 1, ny - 1, x, nx - 1 - x) for x in range(nx)]
    corners = [(y, x) for y in far_rows for x in far_columns]
    pairs = {
        "a": [(at(y, x), at(y ^ 1, x)) for y in range(ny) for x in range(nx)],
        "b": [(at(y, x), at(to_y, to_x)) for y, to_y, x, to_x in second],
        "xa": [(at(y, x), at(y, x ^ 1)) for y in range(ny) for x in range(nx)],
        "xb": [(at(y, x), at(y, beside(x))) for y in range(ny) for x in range(nx) if (y, x) not in corners],
        "relay": [(at(y, x), at(y ^ 1, beside(x))) for y, x in corners],
        "hand_on": [(at(y ^ 1, x), at(y, x)) for y, x in corners],
    }
    cube = P(None, "gy", "gx")
    sheet = P("gy", "gx")
    return jax.shard_map(
        functools.partial(local, pairs, cut),
        mesh=mesh,
        in_specs=(cube,) * 6 + (sheet, sheet),
        out_specs=(cube, cube),
        check_vma=False,
    )
```

```python
import functools

import jax
import jax.numpy as jnp
from jax import lax
from jax.experimental import pallas as pl
from jax.experimental.pallas import tpu as pltpu
from jax.sharding import PartitionSpec as P

thermal_coef = 0.1655
haline_coef = 0.76554
thermal_curve = 0.05952
haline_curve = 0.00054914
thermal_press = 0.0001497
haline_press = 1.109e-05
cabbeling = 0.0024341
bottom_depth = 5800.0
slope_limit = 1.0
strat_offset = 0.1

ROWS = 8
LANES = 128
GRID_AXES = ("gy", "gx")


def padded(levels):
    return -(-(levels + 2) // 8) * 8


def density(temper, saline, strata_height):
    heat_slope = -thermal_coef * (1.0 + thermal_press * strata_height)
    salt_slope = haline_coef * (1.0 - haline_press * strata_height)
    return (
        heat_slope - (0.5 * thermal_coef * thermal_curve) * temper - cabbeling * saline
    ) * temper + (salt_slope - (0.5 * haline_coef * haline_curve) * saline) * saline


def quotient(top, bottom):
    return top / bottom


def face_flux(speed, half_diffus, wet, left, right):
    steps = jnp.maximum(left[5] + right[5], 0.0) + 4.0 * strat_offset
    quarter = jnp.clip(quotient(right[2] - left[2], steps), -0.25 * slope_limit, 0.25 * slope_limit)
    forward = speed > 0.0

    def one(i):
        carried = speed * jnp.where(forward, left[i], right[i])
        mixed = half_diffus * (right[i] - left[i] - quarter * (left[3 + i] + right[3 + i]))
        return jnp.where(wet, carried - mixed, 0.0)

    return one(0), one(1)


def fetch(sources, targets, sems):
    copies = [pltpu.make_async_copy(a, b, sems.at[i]) for i, (a, b) in enumerate(zip(sources, targets))]
    for copy in copies:
        copy.start()
    return copies


def pack_kernel(
    levels, t_hbm, s_hbm, v_hbm, u_hbm, diff_hbm, depth_hbm,
    b_ref, xb_ref, xa_ref, a_ref, t_ref, s_ref, v_ref, u_ref, diff_ref, depth_ref, sems,
):
    copies = fetch(
        (t_hbm, s_hbm, v_hbm, u_hbm, diff_hbm, depth_hbm),
        [ref.at[pl.ds(0, levels)] for ref in (t_ref, s_ref, v_ref, u_ref)] + [diff_ref, depth_ref],
        sems,
    )
    block = padded(levels)
    gy, gx = lax.axis_index("gy"), lax.axis_index("gx")
    y_even, x_even = gy % 2 == 0, gx % 2 == 0
    is_top = gy == lax.axis_size("gy") - 1
    lane = lax.broadcasted_iota(jnp.int32, (block, LANES), 1)
    source = jnp.where(is_top, LANES - 1 - lane, lane)
    one_lane = lax.broadcasted_iota(jnp.int32, (ROWS, LANES), 1)
    copies[4].wait()
    copies[5].wait()
    depth = depth_ref[...].astype(jnp.float32)
    diff = diff_ref[...]
    for ref in (t_ref, s_ref, v_ref, u_ref):
        ref[levels:] = jnp.zeros((block - levels, ROWS, LANES), jnp.float32)
    index = lax.broadcasted_iota(jnp.int32, (block, LANES), 0)

    def row_part(ref, i):
        ref = ref.reshape(block * ROWS, LANES)
        top = ref[pl.ds(ROWS - 1, block, stride=ROWS), :]
        low = ref[pl.ds(0, block, stride=ROWS), :]
        near, far = jnp.where(y_even, top, low), jnp.where(y_even, low, top)
        if i == 0:
            for name, value in ((levels, diff), (levels + 1, depth)):
                near = jnp.where(index == name, jnp.where(y_even, value[ROWS - 1 :], value[:1]), near)
                far = jnp.where(index == name, jnp.where(y_even, value[:1], value[ROWS - 1 :]), far)
        b_ref[i * block : (i + 1) * block] = jnp.take_along_axis(far, source, axis=1, mode="promise_in_bounds")
        if i < 2:
            a_ref[i * block : (i + 1) * block] = near
        else:
            whole = levels // ROWS * ROWS
            a_ref[2 * block :] = near[:whole]
            a_ref[block - (levels - whole) : block] = near[whole:levels]

    def columns(ref, c, first):
        out = jnp.zeros((ROWS, LANES), jnp.float32)
        for k in range(levels):
            moved = pltpu.roll(ref[k], (k - c) % LANES, 1)
            out = jnp.where(one_lane == k, moved, out)
        if first:
            out = jnp.where(one_lane == levels, pltpu.roll(diff, (levels - c) % LANES, 1), out)
            out = jnp.where(one_lane == levels + 1, pltpu.roll(depth, (levels + 1 - c) % LANES, 1), out)
        return out

    def column_part(ref, i):
        east = columns(ref, LANES - 1, i == 0)
        west = columns(ref, 0, i == 0) if i < 2 else jnp.zeros((ROWS, LANES), jnp.float32)
        xa_ref[i * ROWS : (i + 1) * ROWS] = jnp.where(x_even, east, west)
        xb_ref[i * ROWS : (i + 1) * ROWS] = jnp.where(x_even, west, east)

    for i, ref in enumerate((t_ref, s_ref)):
        copies[i].wait()
        row_part(ref, i)
        column_part(ref, i)
    copies[2].wait()
    row_part(v_ref, 2)
    copies[3].wait()
    column_part(u_ref, 2)


def starts_early(gy, gx, cut):
    ny = lax.axis_size("gy")
    return jnp.logical_and(gy < ny // 2, gx % cut < cut // 2)


def early_kernel(levels, group, cut, *refs):
    @pl.when(starts_early(lax.axis_index("gy"), lax.axis_index("gx"), cut))
    def _():
        inner(levels, group, *refs)


def late_kernel(levels, group, cut, *refs):
    n_in, n_out = 8, 7
    ins, outs = refs[:n_in], refs[n_in + n_out :]

    @pl.when(jnp.logical_not(starts_early(lax.axis_index("gy"), lax.axis_index("gx"), cut)))
    def _():
        inner(levels, group, *ins, *outs)


def inner(
    levels, group, t_ref, s_ref, u_ref, v_ref, w_ref, kap_ref, diff_ref, depth_ref,
    star_t_ref, star_s_ref, inv_ref, low_ref, ratio_ref, own_a_ref, own_b_ref,
):
    block = padded(levels)
    depth = depth_ref[...]
    diff = diff_ref[...]
    lane = lax.broadcasted_iota(jnp.int32, (ROWS, LANES), 1)
    row = lax.broadcasted_iota(jnp.int32, (ROWS, LANES), 0)

    def east(x):
        return pltpu.roll(x, LANES - 1, 1)

    def west(x):
        return pltpu.roll(x, 1, 1)

    def north(x):
        return pltpu.roll(x, ROWS - 1, 0)

    def south(x):
        return pltpu.roll(x, 1, 0)

    depth_x = jnp.where(lane == LANES - 1, 0, jnp.minimum(depth, east(depth)))
    depth_y = jnp.where(row == ROWS - 1, 0, jnp.minimum(depth, north(depth)))
    diff_x = 0.5 * (diff + east(diff))
    diff_y = 0.5 * (diff + north(diff))

    def at(ref, k):
        return ref[k]

    def height(k):
        part = (k.astype(jnp.float32) + 0.5) / levels
        return bottom_depth * (part * part)

    def level(k, carry):
        t, s, dens, step_t, step_s, step_d, top_t, top_s = carry
        below = jnp.minimum(k + 1, levels - 1)
        open_below = k + 1 < depth
        t1, s1 = at(t_ref, below), at(s_ref, below)
        dens1 = density(t1, s1, height(below))
        next_t = jnp.where(open_below, t1 - t, 0.0)
        next_s = jnp.where(open_below, s1 - s, 0.0)
        next_d = jnp.where(open_below, dens1 - dens, 0.0)
        w1 = at(w_ref, below)
        up = w1 > 0.0
        low_t = jnp.where(open_below, w1 * jnp.where(up, t1, t), 0.0)
        low_s = jnp.where(open_below, w1 * jnp.where(up, s1, s), 0.0)
        here = (t, s, dens, step_t + next_t, step_s + next_s, step_d + next_d)
        fx_t, fx_s = face_flux(at(u_ref, k), diff_x, k < depth_x, here, tuple(map(east, here)))
        fy_t, fy_s = face_flux(at(v_ref, k), diff_y, k < depth_y, here, tuple(map(north, here)))
        star_t_ref[k] = t - (fx_t - west(fx_t)) - (fy_t - south(fy_t)) - (top_t - low_t)
        star_s_ref[k] = s - (fx_s - west(fx_s)) - (fy_s - south(fy_s)) - (top_s - low_s)
        return t1, s1, dens1, next_t, next_s, next_d, low_t, low_s

    zero = jnp.zeros((ROWS, LANES), jnp.float32)
    t0, s0 = t_ref[0], s_ref[0]
    first = (t0, s0, density(t0, s0, bottom_depth * (0.5 / levels) ** 2), zero, zero, zero, zero, zero)

    middle = levels // 2

    def coupling(k):
        return jnp.where(k < depth, kap_ref[k], 0.0)

    def eliminate(j, carry):
        above, ratio, below, ratio_up = carry
        k = j
        under = coupling(k + 1)
        inv = quotient(1.0, 1.0 + above + under - above * ratio)
        inv_ref[k] = inv
        low_ref[k] = above * inv
        ratio = under * inv
        ratio_ref[k] = ratio
        k = levels - 1 - j
        over = coupling(k)
        inv = quotient(1.0, 1.0 + over + below - below * ratio_up)
        inv_ref[k] = inv
        low_ref[k] = below * inv
        ratio_up = over * inv
        ratio_ref[k] = ratio_up
        return under, ratio, over, ratio_up

    rounds = levels // group
    pairs = -(-middle // rounds)
    whole = middle // pairs

    def both(i, carry):
        one, two = carry
        for j in range(group):
            one = level(i * group + j, one)
            if j < pairs:
                two = eliminate(i * pairs + j, two)
        return one, two

    def some(i, carry):
        for j in range(group):
            carry = level(i * group + j, carry)
        return carry

    carry, elimination = lax.fori_loop(0, whole, both, (first, (zero, zero, zero, zero)))
    lax.fori_loop(whole, rounds, some, carry)
    for j in range(whole * pairs, middle):
        elimination = eliminate(jnp.int32(j), elimination)
    above, ratio, below, ratio_up = elimination
    inv = 1.0 / (1.0 + above + below - above * ratio - below * ratio_up)
    inv_ref[middle] = inv
    low_ref[middle] = above * inv
    ratio_ref[middle] = below * inv

    gy = lax.axis_index("gy")
    y_even = gy % 2 == 0
    depth_f = depth.astype(jnp.float32)
    index = lax.broadcasted_iota(jnp.int32, (block, LANES), 0)
    for i, ref in enumerate((t_ref, s_ref, v_ref)):
        flat = ref.reshape(block * ROWS, LANES)
        top = flat[pl.ds(ROWS - 1, block, stride=ROWS), :]
        low = flat[pl.ds(0, block, stride=ROWS), :]
        for own_ref, keep_top in ((own_a_ref, y_even), (own_b_ref, jnp.logical_not(y_even))):
            own = jnp.where(keep_top, top, low)
            if i == 0:
                for name, value in ((levels, diff), (levels + 1, depth_f)):
                    own = jnp.where(index == name, jnp.where(keep_top, value[ROWS - 1 :], value[:1]), own)
            own_ref[i * block : (i + 1) * block] = own


def column_sums(x, open_here, axis):
    size = x.shape[axis]
    step = jnp.where(open_here, x - pltpu.roll(x, 1, axis), 0.0)
    return step + pltpu.roll(step, size - 1, axis)


def side(temper, saline, depth, index, heights, axis):
    dens = density(temper, saline, heights)
    open_here = jnp.logical_and(index >= 1, index < depth)
    return (
        temper,
        saline,
        dens,
        column_sums(temper, open_here, axis),
        column_sums(saline, open_here, axis),
        column_sums(dens, open_here, axis),
    )


def edge_flux(levels, axis, index, own, got, own_left, fold):
    part = (index.astype(jnp.float32) + 0.5) / levels
    heights = bottom_depth * (part * part)
    left = [jnp.where(own_left, o, g) for o, g in zip(own, got)]
    right = [jnp.where(own_left, g, o) for o, g in zip(own, got)]
    speed = left[2]
    if fold is not None:
        speed = jnp.where(fold, 0.5 * (own[2] - got[2]), speed)
    wet = index.astype(jnp.float32) < jnp.minimum(left[4], right[4])
    level = index.astype(jnp.float32)
    return face_flux(
        speed,
        0.5 * (left[3] + right[3]),
        wet,
        side(left[0], left[1], left[4], level, heights, axis),
        side(right[0], right[1], right[4], level, heights, axis),
    )


def final_kernel(
    levels, cut, got_b, got_relay, got_xb, got_xa, got_a, own_a, own_b, own_xa, own_xb,
    star_t_ref, star_s_ref, inv_ref, low_ref, ratio_ref,
    out_t_ref, out_s_ref, north_ref, south_ref,
):
    block = padded(levels)
    gy, gx = lax.axis_index("gy"), lax.axis_index("gx")
    y_even, x_even = gy % 2 == 0, gx % 2 == 0
    y_odd, x_odd = jnp.logical_not(y_even), jnp.logical_not(x_even)
    is_top = gy == lax.axis_size("gy") - 1

    index = lax.broadcasted_iota(jnp.int32, (block, LANES), 0)

    corner = jnp.logical_and(is_far_row(gy), is_far_column(gx, cut))

    def rows(ref):
        t, s, q = (ref[i * block : (i + 1) * block] for i in range(3))
        return t, s, q, t[levels : levels + 1], t[levels + 1 : levels + 2]

    whole = levels // ROWS * ROWS
    t, s = got_a[:block], got_a[block : 2 * block]
    q = jnp.concatenate(
        [got_a[2 * block :], t[block - (levels - whole) :], jnp.zeros((block - levels, LANES), jnp.float32)], 0
    )
    near = t, s, q, t[levels : levels + 1], t[levels + 1 : levels + 2]
    flux_a = edge_flux(levels, 0, index, rows(own_a), near, y_even, None)
    flux_b = edge_flux(levels, 0, index, rows(own_b), rows(got_b), y_odd, is_top)
    for i in range(2):
        north_ref[i] = -jnp.where(y_even, flux_a[i], flux_b[i])
        south_ref[i] = jnp.where(y_even, flux_b[i], flux_a[i])

    lane = lax.broadcasted_iota(jnp.int32, (ROWS, LANES), 1)
    row = lax.broadcasted_iota(jnp.int32, (ROWS, LANES), 0)

    def cols(ref, other=None):
        t, s, q = (
            ref[i * ROWS : (i + 1) * ROWS]
            if other is None
            else jnp.where(corner, other[i * ROWS : (i + 1) * ROWS], ref[i * ROWS : (i + 1) * ROWS])
            for i in range(3)
        )
        return t, s, q, t[:, levels : levels + 1], t[:, levels + 1 : levels + 2]

    flux_xa = edge_flux(levels, 1, lane, cols(own_xa), cols(got_xa), x_even, None)
    flux_xb = edge_flux(levels, 1, lane, cols(own_xb), cols(got_xb, got_relay), x_odd, None)
    east = [-jnp.where(x_even, flux_xa[i], flux_xb[i]) for i in range(2)]
    west = [jnp.where(x_even, flux_xb[i], flux_xa[i]) for i in range(2)]
    last_lane, first_lane = lane == LANES - 1, lane == 0
    last_row, first_row = row == ROWS - 1, row == 0

    def right_side(i, k):
        ref = (star_t_ref, star_s_ref)[i]
        x_part = jnp.where(
            last_lane,
            pltpu.roll(east[i], (LANES - 1 - k) % LANES, 1),
            jnp.where(first_lane, pltpu.roll(west[i], (-k) % LANES, 1), 0.0),
        )
        y_part = jnp.where(
            last_row,
            north_ref[i, k : k + 1, :],
            jnp.where(first_row, south_ref[i, k : k + 1, :], 0.0),
        )
        return (ref[k] + (x_part + y_part)) * inv_ref[k]

    outs = (out_t_ref, out_s_ref)
    middle = levels // 2
    zero = jnp.zeros((ROWS, LANES), jnp.float32)
    upper, lower = [zero, zero], [zero, zero]
    for j in range(middle):
        for i in range(2):
            upper[i] = right_side(i, j) + low_ref[j] * upper[i]
            outs[i][j] = upper[i]
            k = levels - 1 - j
            lower[i] = right_side(i, k) + low_ref[k] * lower[i]
            outs[i][k] = lower[i]
    for i in range(2):
        solved = right_side(i, middle) + low_ref[middle] * upper[i] + ratio_ref[middle] * lower[i]
        outs[i][middle] = solved
        upper[i] = lower[i] = solved
    for j in range(1, middle + 1):
        for i in range(2):
            k = middle - j
            upper[i] = outs[i][k] + ratio_ref[k] * upper[i]
            outs[i][k] = upper[i]
            k = middle + j
            lower[i] = outs[i][k] + ratio_ref[k] * lower[i]
            outs[i][k] = lower[i]


def call(kernel, outs, operands, memory, scratch=(), flops=0, name=None, aliases=None):
    return pl.pallas_call(
        kernel,
        out_shape=[jax.ShapeDtypeStruct(getattr(s, "shape", s), getattr(s, "dtype", jnp.float32)) for s in outs],
        in_specs=[pl.BlockSpec(memory_space=memory)] * len(operands),
        out_specs=[pl.BlockSpec(memory_space=pltpu.VMEM)] * len(outs),
        scratch_shapes=list(scratch),
        input_output_aliases=aliases or {},
        compiler_params=pltpu.CompilerParams(vmem_limit_bytes=24 * 1024 * 1024),
        cost_estimate=pl.CostEstimate(flops=flops, bytes_accessed=4 * 1024 * 1024, transcendentals=0),
        name=name,
    )(*operands)


def local(pairs, cut, heat, salt, u, v, w, kap, diff, depth):
    levels, rows, lanes = heat.shape
    block = padded(levels)
    cube, wide, thin = (levels, rows, lanes), (3 * block, lanes), (3 * rows, lanes)
    compact = (2 * block + levels // rows * rows, lanes)

    def moved(x, which):
        return lax.ppermute(x, GRID_AXES, pairs[which])

    operands = tuple(pltpu.with_memory_space_constraint(x, pltpu.HBM) for x in (heat, salt, v, u, diff, depth))
    pack_b, pack_xb, pack_xa, pack_a, heat, salt, v, u, diff, depth = call(
        functools.partial(pack_kernel, levels), [wide, thin, thin, compact] + [(block, rows, lanes)] * 4 + [diff.shape, depth],
        operands, pltpu.HBM, [pltpu.SemaphoreType.DMA((6,))], name="pack",
    )
    group = next(g for g in (5, 3, 2, 1) if levels % g == 0)
    operands = (heat, salt, u, v, w, kap, diff, depth)
    results = [cube] * 5 + [wide, wide]
    early = list(
        call(functools.partial(early_kernel, levels, group, cut), results, operands, pltpu.VMEM, name="early")
    )
    pack_b, early[0] = lax.optimization_barrier((pack_b, early[0]))
    got_b = moved(pack_b, "b")
    relayed = moved(pack_xb, "relay")
    got_xb = moved(pack_xb, "xb")
    got_xa = moved(pack_xa, "xa")
    got_a = moved(pack_a, "a")
    star_t, star_s, inv, low, ratio, own_a, own_b = call(
        functools.partial(late_kernel, levels, group, cut), results, operands + tuple(early), pltpu.VMEM,
        flops=1_142_000_000, name="late", aliases={8 + i: i for i in range(7)},
    )
    relayed, star_t = lax.optimization_barrier((relayed, star_t))
    got_relay = moved(relayed, "hand_on")
    operands = (
        got_b, got_relay, got_xb, got_xa, got_a, own_a, own_b, pack_xa, pack_xb,
        star_t, star_s, inv, low, ratio,
    )
    return call(
        functools.partial(final_kernel, levels, cut),
        [cube] * 2, operands, pltpu.VMEM, [pltpu.VMEM((2, block, lanes), jnp.float32)] * 2, name="final",
    )


def is_far_row(y):
    ny = lax.axis_size("gy")
    return (y == ny // 2 - 1) | (y == ny // 2) | (y == ny - 1)


def is_far_column(x, cut):
    return (x % cut == 0) | (x % cut == cut - 1)


def solution(mesh):
    ny, nx = mesh.shape["gy"], mesh.shape["gx"]
    cut = nx // 4
    far_rows = (ny // 2 - 1, ny // 2, ny - 1)
    far_columns = [x for x in range(nx) if x % cut in (0, cut - 1)]

    def at(y, x):
        return y * nx + x

    def beside(x):
        return (((x + 1) ^ 1) - 1) % nx

    second = [(y, ((y + 1) ^ 1) - 1, x, x) for y in range(1, ny - 1) for x in range(nx)]
    second += [(ny - 1, ny - 1, x, nx - 1 - x) for x in range(nx)]
    corners = [(y, x) for y in far_rows for x in far_columns]
    pairs = {
        "a": [(at(y, x), at(y ^ 1, x)) for y in range(ny) for x in range(nx)],
        "b": [(at(y, x), at(to_y, to_x)) for y, to_y, x, to_x in second],
        "xa": [(at(y, x), at(y, x ^ 1)) for y in range(ny) for x in range(nx)],
        "xb": [(at(y, x), at(y, beside(x))) for y in range(ny) for x in range(nx) if (y, x) not in corners],
        "relay": [(at(y, x), at(y ^ 1, beside(x))) for y, x in corners],
        "hand_on": [(at(y ^ 1, x), at(y, x)) for y, x in corners],
    }
    cube = P(None, "gy", "gx")
    sheet = P("gy", "gx")
    return jax.shard_map(
        functools.partial(local, pairs, cut),
        mesh=mesh,
        in_specs=(cube,) * 6 + (sheet, sheet),
        out_specs=(cube, cube),
        check_vma=False,
    )
```

```python
import functools

import jax
import jax.numpy as jnp
from jax import lax
from jax.experimental import pallas as pl
from jax.experimental.pallas import tpu as pltpu
from jax.sharding import PartitionSpec as P

thermal_coef = 0.1655
haline_coef = 0.76554
thermal_curve = 0.05952
haline_curve = 0.00054914
thermal_press = 0.0001497
haline_press = 1.109e-05
cabbeling = 0.0024341
bottom_depth = 5800.0
slope_limit = 1.0
strat_offset = 0.1

ROWS = 8
LANES = 128
GRID_AXES = ("gy", "gx")


def padded(levels):
    return -(-(levels + 2) // 8) * 8


def density(temper, saline, strata_height):
    heat_slope = -thermal_coef * (1.0 + thermal_press * strata_height)
    salt_slope = haline_coef * (1.0 - haline_press * strata_height)
    return (
        heat_slope - (0.5 * thermal_coef * thermal_curve) * temper - cabbeling * saline
    ) * temper + (salt_slope - (0.5 * haline_coef * haline_curve) * saline) * saline


def quotient(top, bottom):
    return top / bottom


def face_flux(speed, half_diffus, wet, left, right):
    steps = jnp.maximum(left[5] + right[5], 0.0) + 4.0 * strat_offset
    quarter = jnp.clip(quotient(right[2] - left[2], steps), -0.25 * slope_limit, 0.25 * slope_limit)
    forward = speed > 0.0

    def one(i):
        carried = speed * jnp.where(forward, left[i], right[i])
        mixed = half_diffus * (right[i] - left[i] - quarter * (left[3 + i] + right[3 + i]))
        return jnp.where(wet, carried - mixed, 0.0)

    return one(0), one(1)


def fetch(sources, targets, sems):
    copies = [pltpu.make_async_copy(a, b, sems.at[i]) for i, (a, b) in enumerate(zip(sources, targets))]
    for copy in copies:
        copy.start()
    return copies


def pack_kernel(
    levels, t_hbm, s_hbm, v_hbm, u_hbm, diff_hbm, depth_hbm,
    b_ref, xb_ref, xa_ref, a_ref, own_xa_ref, own_xb_ref, t_ref, s_ref, v_ref, u_ref, diff_ref, depth_ref, sems,
):
    copies = fetch(
        (t_hbm, s_hbm, v_hbm, u_hbm, diff_hbm, depth_hbm),
        [ref.at[pl.ds(0, levels)] for ref in (t_ref, s_ref, v_ref, u_ref)] + [diff_ref, depth_ref],
        sems,
    )
    block = padded(levels)
    gy, gx = lax.axis_index("gy"), lax.axis_index("gx")
    y_even, x_even = gy % 2 == 0, gx % 2 == 0
    is_top = gy == lax.axis_size("gy") - 1
    lane = lax.broadcasted_iota(jnp.int32, (block, LANES), 1)
    source = jnp.where(is_top, LANES - 1 - lane, lane)
    one_lane = lax.broadcasted_iota(jnp.int32, (ROWS, LANES), 1)
    copies[4].wait()
    copies[5].wait()
    depth = depth_ref[...].astype(jnp.float32)
    diff = diff_ref[...]
    for ref in (t_ref, s_ref, v_ref, u_ref):
        ref[levels:] = jnp.zeros((block - levels, ROWS, LANES), jnp.float32)
    index = lax.broadcasted_iota(jnp.int32, (block, LANES), 0)

    def row_part(ref, i):
        ref = ref.reshape(block * ROWS, LANES)
        top = ref[pl.ds(ROWS - 1, block, stride=ROWS), :]
        low = ref[pl.ds(0, block, stride=ROWS), :]
        near, far = jnp.where(y_even, top, low), jnp.where(y_even, low, top)
        if i == 0:
            for name, value in ((levels, diff), (levels + 1, depth)):
                near = jnp.where(index == name, jnp.where(y_even, value[ROWS - 1 :], value[:1]), near)
                far = jnp.where(index == name, jnp.where(y_even, value[:1], value[ROWS - 1 :]), far)
        b_ref[i * block : (i + 1) * block] = jnp.take_along_axis(far, source, axis=1, mode="promise_in_bounds")
        if i < 2:
            a_ref[i * block : (i + 1) * block] = near
        else:
            whole = levels // ROWS * ROWS
            a_ref[2 * block :] = near[:whole]
            a_ref[block - (levels - whole) : block] = near[whole:levels]

    def column_part(ref, i):
        planes = [ref[k] for k in range(levels)]
        if i == 0:
            planes += [diff, depth]
        zero = jnp.zeros((ROWS, LANES), jnp.float32)
        east, west = [zero] * 4, [zero] * 4
        for k, plane in enumerate(planes):
            moved = pltpu.roll(plane, k + 1, 1)
            east[k % 4] = jnp.where(one_lane == k, moved, east[k % 4])
            if i < 2:
                west[k % 4] = jnp.where(one_lane == k + 1, moved, west[k % 4])
        east = (east[0] + east[1]) + (east[2] + east[3])
        west = (west[0] + west[1]) + (west[2] + west[3])
        part = slice(i * ROWS, (i + 1) * ROWS)
        own_xa_ref[part] = jnp.where(x_even, east, west)
        own_xb_ref[part] = jnp.where(x_even, west, east)
        east, west = pltpu.roll(east, 1, 1), pltpu.roll(west, LANES - 1, 1)
        xa_ref[part] = jnp.where(x_even, east, west)
        xb_ref[part] = jnp.where(x_even, west, east)

    copies[0].wait()
    copies[1].wait()
    for i, ref in enumerate((t_ref, s_ref)):
        row_part(ref, i)
        column_part(ref, i)
    copies[2].wait()
    copies[3].wait()
    row_part(v_ref, 2)
    column_part(u_ref, 2)


def starts_early(gy, gx, cut):
    ny = lax.axis_size("gy")
    return jnp.logical_and(gy < ny // 2, gx % cut < cut // 2)


def early_kernel(levels, group, cut, *refs):
    @pl.when(starts_early(lax.axis_index("gy"), lax.axis_index("gx"), cut))
    def _():
        inner(levels, group, *refs)


def late_kernel(levels, group, cut, *refs):
    n_in, n_out = 10, 9
    ins, outs = refs[:n_in], refs[n_in + n_out :]

    @pl.when(jnp.logical_not(starts_early(lax.axis_index("gy"), lax.axis_index("gx"), cut)))
    def _():
        inner(levels, group, *ins, *outs)


def inner(
    levels, group, t_ref, s_ref, u_ref, v_ref, w_ref, kap_ref, diff_ref, depth_ref,
    own_xa_ref, own_xb_ref, star_t_ref, star_s_ref, inv_ref, low_ref, ratio_ref, own_a_ref, own_b_ref,
    side_xa_ref, side_xb_ref,
):
    block = padded(levels)
    depth = depth_ref[...]
    diff = diff_ref[...]
    lane = lax.broadcasted_iota(jnp.int32, (ROWS, LANES), 1)
    row = lax.broadcasted_iota(jnp.int32, (ROWS, LANES), 0)

    def east(x):
        return pltpu.roll(x, LANES - 1, 1)

    def west(x):
        return pltpu.roll(x, 1, 1)

    def north(x):
        return pltpu.roll(x, ROWS - 1, 0)

    def south(x):
        return pltpu.roll(x, 1, 0)

    depth_x = jnp.where(lane == LANES - 1, 0, jnp.minimum(depth, east(depth)))
    depth_y = jnp.where(row == ROWS - 1, 0, jnp.minimum(depth, north(depth)))
    diff_x = 0.5 * (diff + east(diff))
    diff_y = 0.5 * (diff + north(diff))

    def at(ref, k):
        return ref[k]

    def height(k):
        part = (k.astype(jnp.float32) + 0.5) / levels
        return bottom_depth * (part * part)

    def level(k, carry):
        t, s, dens, step_t, step_s, step_d, top_t, top_s = carry
        below = jnp.minimum(k + 1, levels - 1)
        open_below = k + 1 < depth
        t1, s1 = at(t_ref, below), at(s_ref, below)
        dens1 = density(t1, s1, height(below))
        next_t = jnp.where(open_below, t1 - t, 0.0)
        next_s = jnp.where(open_below, s1 - s, 0.0)
        next_d = jnp.where(open_below, dens1 - dens, 0.0)
        w1 = at(w_ref, below)
        up = w1 > 0.0
        low_t = jnp.where(open_below, w1 * jnp.where(up, t1, t), 0.0)
        low_s = jnp.where(open_below, w1 * jnp.where(up, s1, s), 0.0)
        here = (t, s, dens, step_t + next_t, step_s + next_s, step_d + next_d)
        fx_t, fx_s = face_flux(at(u_ref, k), diff_x, k < depth_x, here, tuple(map(east, here)))
        fy_t, fy_s = face_flux(at(v_ref, k), diff_y, k < depth_y, here, tuple(map(north, here)))
        star_t_ref[k] = t - (fx_t - west(fx_t)) - (fy_t - south(fy_t)) - (top_t - low_t)
        star_s_ref[k] = s - (fx_s - west(fx_s)) - (fy_s - south(fy_s)) - (top_s - low_s)
        return t1, s1, dens1, next_t, next_s, next_d, low_t, low_s

    zero = jnp.zeros((ROWS, LANES), jnp.float32)
    t0, s0 = t_ref[0], s_ref[0]
    first = (t0, s0, density(t0, s0, bottom_depth * (0.5 / levels) ** 2), zero, zero, zero, zero, zero)

    middle = levels // 2

    def coupling(k):
        return jnp.where(k < depth, kap_ref[k], 0.0)

    def eliminate(j, carry):
        above, ratio, below, ratio_up = carry
        k = j
        under = coupling(k + 1)
        inv = quotient(1.0, 1.0 + above + under - above * ratio)
        inv_ref[k] = inv
        low_ref[k] = above * inv
        ratio = under * inv
        ratio_ref[k] = ratio
        k = levels - 1 - j
        over = coupling(k)
        inv = quotient(1.0, 1.0 + over + below - below * ratio_up)
        inv_ref[k] = inv
        low_ref[k] = below * inv
        ratio_up = over * inv
        ratio_ref[k] = ratio_up
        return under, ratio, over, ratio_up

    rounds = levels // group
    pairs = -(-middle // rounds)
    whole = middle // pairs

    def both(i, carry):
        one, two = carry
        for j in range(group):
            one = level(i * group + j, one)
            if j < pairs:
                two = eliminate(i * pairs + j, two)
        return one, two

    def some(i, carry):
        for j in range(group):
            carry = level(i * group + j, carry)
        return carry

    carry, elimination = lax.fori_loop(0, whole, both, (first, (zero, zero, zero, zero)))
    lax.fori_loop(whole, rounds, some, carry)
    for j in range(whole * pairs, middle):
        elimination = eliminate(jnp.int32(j), elimination)
    above, ratio, below, ratio_up = elimination
    inv = 1.0 / (1.0 + above + below - above * ratio - below * ratio_up)
    inv_ref[middle] = inv
    low_ref[middle] = above * inv
    ratio_ref[middle] = below * inv

    gy = lax.axis_index("gy")
    y_even = gy % 2 == 0
    depth_f = depth.astype(jnp.float32)
    index = lax.broadcasted_iota(jnp.int32, (block, LANES), 0)
    heights = level_heights(index, levels)
    flats = [ref.reshape(block * ROWS, LANES) for ref in (t_ref, s_ref, v_ref)]
    tops = [flat[pl.ds(ROWS - 1, block, stride=ROWS), :] for flat in flats]
    lows = [flat[pl.ds(0, block, stride=ROWS), :] for flat in flats]
    for own_ref, keep_top in ((own_a_ref, y_even), (own_b_ref, jnp.logical_not(y_even))):
        t, s, q = (jnp.where(keep_top, top, low) for top, low in zip(tops, lows))
        edge_diff, edge_depth = (
            jnp.where(keep_top, value[ROWS - 1 :], value[:1]) for value in (diff, depth_f)
        )
        for i, field in enumerate(side(t, s, edge_depth, index.astype(jnp.float32), heights, 0) + (q,)):
            if i == 0:
                field = jnp.where(index == levels, edge_diff, jnp.where(index == levels + 1, edge_depth, field))
            own_ref[i * block : (i + 1) * block] = field
    x_even = lax.axis_index("gx") % 2 == 0
    for own_ref, side_ref, own_left in ((own_xa_ref, side_xa_ref, x_even), (own_xb_ref, side_xb_ref, jnp.logical_not(x_even))):
        t, s, q = (own_ref[i * ROWS : (i + 1) * ROWS] for i in range(3))
        ahead = jnp.where(own_left, 0, 1)
        values = column_side(t, s, levels, ahead) + (q,) + edge_values(t, levels, ahead)
        for i, value in enumerate(values):
            side_ref[i * ROWS : (i + 1) * ROWS] = value


def level_heights(index, levels):
    part = (index.astype(jnp.float32) + 0.5) / levels
    return bottom_depth * (part * part)


def column_sums(x, open_here, axis):
    size = x.shape[axis]
    step = jnp.where(open_here, x - pltpu.roll(x, 1, axis), 0.0)
    return step + pltpu.roll(step, size - 1, axis)


def side(temper, saline, depth, index, heights, axis):
    dens = density(temper, saline, heights)
    open_here = jnp.logical_and(index >= 1, index < depth)
    return (
        temper,
        saline,
        dens,
        column_sums(temper, open_here, axis),
        column_sums(saline, open_here, axis),
        column_sums(dens, open_here, axis),
    )


def edge_values(t, levels, ahead):
    one, two, three = (t[:, levels + i : levels + i + 1] for i in range(3))
    first, second = jnp.where(ahead == 0, one, two), jnp.where(ahead == 0, two, three)
    return jnp.broadcast_to(first, t.shape), jnp.broadcast_to(second, t.shape)


def column_side(t, s, levels, ahead):
    depth = edge_values(t, levels, ahead)[1]
    level = lax.broadcasted_iota(jnp.int32, t.shape, 1) - ahead
    here, over, under = (
        (
            pltpu.roll(t, shift, 1) if shift else t,
            pltpu.roll(s, shift, 1) if shift else s,
            level_heights(level - move, levels),
        )
        for shift, move in ((0, 0), (1, 1), (LANES - 1, -1))
    )
    level = level.astype(jnp.float32)
    open_here = jnp.logical_and(level >= 1.0, level < depth)
    open_under = level + 1.0 < depth
    here, over, under = (x[:2] + (density(*x),) for x in (here, over, under))
    sums = tuple(
        jnp.where(open_here, h - o, 0.0) + jnp.where(open_under, u - h, 0.0) for h, o, u in zip(here, over, under)
    )
    return here + sums


def edge_change(own, got, own_speed, got_speed, diffus, wet, own_left, fold=None):
    sign = jnp.where(own_left, 1.0, -1.0)
    speed = jnp.where(own_left, own_speed, got_speed)
    if fold is not None:
        speed = jnp.where(fold, 0.5 * (own_speed - got_speed), speed)
    outward = sign * speed
    steps = jnp.maximum(own[5] + got[5], 0.0) + 4.0 * strat_offset
    quarter = jnp.clip(quotient(got[2] - own[2], steps), -0.25 * slope_limit, 0.25 * slope_limit)
    leaves = outward > 0.0

    def one(i):
        carried = outward * jnp.where(leaves, own[i], got[i])
        mixed = diffus * (got[i] - own[i] - quarter * (own[3 + i] + got[3 + i]))
        return jnp.where(wet, mixed - carried, 0.0)

    return one(0), one(1)


def final_kernel(
    levels, cut, got_direct, got_b, got_relay, got_xb, got_xa, got_a, own_a, own_b, side_xa, side_xb, _,
    star_t_ref, star_s_ref, inv_ref, low_ref, ratio_ref,
    out_t_ref, out_s_ref, change_ref,
):
    block = padded(levels)
    gy, gx = lax.axis_index("gy"), lax.axis_index("gx")
    y_even, x_even = gy % 2 == 0, gx % 2 == 0
    y_odd, x_odd = jnp.logical_not(y_even), jnp.logical_not(x_even)
    is_top = gy == lax.axis_size("gy") - 1
    corner = jnp.logical_and(is_far_row(gy), is_far_column(gx, cut))
    straight = jnp.logical_and(gy < lax.axis_size("gy") // 2, gx % cut == 0)

    index = lax.broadcasted_iota(jnp.int32, (block, LANES), 0)
    height = level_heights(index, levels)
    level = index.astype(jnp.float32)

    def row_change(place, own_ref, t, s, q, own_left, fold):
        own = [own_ref[i * block : (i + 1) * block] for i in range(7)]
        diffus, depth = t[levels : levels + 1], t[levels + 1 : levels + 2]
        own_diffus, own_depth = own[0][levels : levels + 1], own[0][levels + 1 : levels + 2]
        changes = edge_change(
            own, side(t, s, depth, level, height, 0), own[6], q,
            0.5 * (own_diffus + diffus), level < jnp.minimum(own_depth, depth), own_left, fold,
        )
        for i in range(2):
            change_ref[place, i] = changes[i]

    whole = levels // ROWS * ROWS
    t, s = got_a[:block], got_a[block : 2 * block]
    q = jnp.concatenate(
        [got_a[2 * block :], t[block - (levels - whole) :], jnp.zeros((block - levels, LANES), jnp.float32)], 0
    )
    row_change(0, own_a, t, s, q, y_even, None)
    row_change(1, own_b, *(got_b[i * block : (i + 1) * block] for i in range(3)), y_odd, is_top)

    lane = lax.broadcasted_iota(jnp.int32, (ROWS, LANES), 1)
    row = lax.broadcasted_iota(jnp.int32, (ROWS, LANES), 0)

    def column_change(side_ref, got, own_left):
        own = [side_ref[i * ROWS : (i + 1) * ROWS] for i in range(9)]
        ahead = jnp.where(own_left, 0, 1)
        diffus, depth = edge_values(got[0], levels, ahead)
        level = (lane - ahead).astype(jnp.float32)
        wet = jnp.logical_and(level >= 0.0, level < jnp.minimum(own[8], depth))
        return edge_change(
            own, column_side(got[0], got[1], levels, ahead), own[6], got[2], 0.5 * (own[7] + diffus), wet, own_left
        )

    def thirds(ref):
        return [ref[i * ROWS : (i + 1) * ROWS] for i in range(3)]

    change_xa = column_change(side_xa, thirds(got_xa), x_even)
    from_xb = [
        jnp.where(corner, jnp.where(straight, a, b), c)
        for a, b, c in zip(thirds(got_direct), thirds(got_relay), thirds(got_xb))
    ]
    change_xb = column_change(side_xb, from_xb, x_odd)
    even_lane = lane % 2 == 0
    paired = []
    for i in range(2):
        last = jnp.where(x_even, change_xa[i], change_xb[i])
        first = jnp.where(x_even, change_xb[i], change_xa[i])
        paired.append((jnp.where(even_lane, last, first), jnp.where(even_lane, first, last)))
    at_side = jnp.logical_or(lane == 0, lane == LANES - 1)
    row_a = row == jnp.where(y_even, ROWS - 1, 0)
    row_b = row == jnp.where(y_even, 0, ROWS - 1)

    def right_side(i, k):
        ref = (star_t_ref, star_s_ref)[i]
        x_part = jnp.where(at_side, pltpu.roll(paired[i][k % 2], (LANES - 1 - k) % LANES, 1), 0.0)
        y_part = jnp.where(
            row_a, change_ref[0, i, k : k + 1, :], jnp.where(row_b, change_ref[1, i, k : k + 1, :], 0.0)
        )
        return (ref[k] + (x_part + y_part)) * inv_ref[k]

    outs = (out_t_ref, out_s_ref)
    middle = levels // 2
    zero = jnp.zeros((ROWS, LANES), jnp.float32)
    upper, lower = [zero, zero], [zero, zero]
    for j in range(middle):
        for i in range(2):
            upper[i] = right_side(i, j) + low_ref[j] * upper[i]
            outs[i][j] = upper[i]
            k = levels - 1 - j
            lower[i] = right_side(i, k) + low_ref[k] * lower[i]
            outs[i][k] = lower[i]
    for i in range(2):
        solved = right_side(i, middle) + low_ref[middle] * upper[i] + ratio_ref[middle] * lower[i]
        outs[i][middle] = solved
        upper[i] = lower[i] = solved
    for j in range(1, middle + 1):
        for i in range(2):
            k = middle - j
            upper[i] = outs[i][k] + ratio_ref[k] * upper[i]
            outs[i][k] = upper[i]
            k = middle + j
            lower[i] = outs[i][k] + ratio_ref[k] * lower[i]
            outs[i][k] = lower[i]


def call(kernel, outs, operands, memory, scratch=(), flops=0, name=None, aliases=None):
    return pl.pallas_call(
        kernel,
        out_shape=[jax.ShapeDtypeStruct(getattr(s, "shape", s), getattr(s, "dtype", jnp.float32)) for s in outs],
        in_specs=[pl.BlockSpec(memory_space=memory)] * len(operands),
        out_specs=[pl.BlockSpec(memory_space=pltpu.VMEM)] * len(outs),
        scratch_shapes=list(scratch),
        input_output_aliases=aliases or {},
        compiler_params=pltpu.CompilerParams(vmem_limit_bytes=24 * 1024 * 1024),
        cost_estimate=pl.CostEstimate(flops=flops, bytes_accessed=4 * 1024 * 1024, transcendentals=0),
        name=name,
    )(*operands)


def local(pairs, cut, heat, salt, u, v, w, kap, diff, depth):
    levels, rows, lanes = heat.shape
    block = padded(levels)
    cube, wide, thin = (levels, rows, lanes), (3 * block, lanes), (3 * rows, lanes)
    compact = (2 * block + levels // rows * rows, lanes)

    def moved(x, which):
        return lax.ppermute(x, GRID_AXES, pairs[which])

    operands = tuple(pltpu.with_memory_space_constraint(x, pltpu.HBM) for x in (heat, salt, v, u, diff, depth))
    pack_b, pack_xb, pack_xa, pack_a, own_xa, own_xb, heat, salt, v, u, diff, depth = call(
        functools.partial(pack_kernel, levels), [wide, thin, thin, compact, thin, thin] + [(block, rows, lanes)] * 4 + [diff.shape, depth],
        operands, pltpu.HBM, [pltpu.SemaphoreType.DMA((6,))], name="pack",
    )
    group = next(g for g in (5, 3, 2, 1) if levels % g == 0)
    operands = (heat, salt, u, v, w, kap, diff, depth, own_xa, own_xb)
    results = [cube] * 5 + [(7 * block, lanes)] * 2 + [(9 * rows, lanes)] * 2
    early = list(
        call(functools.partial(early_kernel, levels, group, cut), results, operands, pltpu.VMEM, name="early")
    )
    direct = moved(pack_xb, "direct")
    pack_b, early[0] = lax.optimization_barrier((pack_b, early[0]))
    got_b = moved(pack_b, "b")
    relayed = moved(pack_xb, "relay")
    got_xb = moved(pack_xb, "xb")
    got_xa = moved(pack_xa, "xa")
    got_a = moved(pack_a, "a")
    direct, early[0] = lax.optimization_barrier((direct, early[0]))
    star_t, star_s, inv, low, ratio, own_a, own_b, side_xa, side_xb = call(
        functools.partial(late_kernel, levels, group, cut), results, operands + tuple(early), pltpu.VMEM,
        flops=1_145_000_000, name="late", aliases={10 + i: i for i in range(9)},
    )
    relayed, star_t = lax.optimization_barrier((relayed, star_t))
    got_relay = moved(relayed, "hand_on")
    operands = (
        direct, got_b, got_relay, got_xb, got_xa, got_a, own_a, own_b, side_xa, side_xb, pack_xa,
        star_t, star_s, inv, low, ratio,
    )
    return call(
        functools.partial(final_kernel, levels, cut),
        [cube] * 2, operands, pltpu.VMEM, [pltpu.VMEM((2, 2, block, lanes), jnp.float32)], name="final",
    )


def is_far_row(y):
    ny = lax.axis_size("gy")
    return (y == ny // 2 - 1) | (y == ny // 2) | (y == ny - 1)


def is_far_column(x, cut):
    return (x % cut == 0) | (x % cut == cut - 1)


def solution(mesh):
    ny, nx = mesh.shape["gy"], mesh.shape["gx"]
    cut = nx // 4
    far_rows = (ny // 2 - 1, ny // 2, ny - 1)
    far_columns = [x for x in range(nx) if x % cut in (0, cut - 1)]

    def at(y, x):
        return y * nx + x

    def beside(x):
        return (((x + 1) ^ 1) - 1) % nx

    second = [(y, ((y + 1) ^ 1) - 1, x, x) for y in range(1, ny - 1) for x in range(nx)]
    second += [(ny - 1, ny - 1, x, nx - 1 - x) for x in range(nx)]
    corners = [(y, x) for y in far_rows for x in far_columns]
    pairs = {
        "a": [(at(y, x), at(y ^ 1, x)) for y in range(ny) for x in range(nx)],
        "b": [(at(y, x), at(to_y, to_x)) for y, to_y, x, to_x in second],
        "xa": [(at(y, x), at(y, x ^ 1)) for y in range(ny) for x in range(nx)],
        "xb": [(at(y, x), at(y, beside(x))) for y in range(ny) for x in range(nx) if (y, x) not in corners],
        "direct": [(at(y, x), at(y, beside(x))) for y, x in corners if y < ny // 2 and x % cut == cut - 1],
        "relay": [(at(y, x), at(y ^ 1, beside(x))) for y, x in corners if y >= ny // 2 or x % cut == 0],
        "hand_on": [(at(y ^ 1, x), at(y, x)) for y, x in corners if y >= ny // 2 or x % cut == cut - 1],
    }
    cube = P(None, "gy", "gx")
    sheet = P("gy", "gx")
    return jax.shard_map(
        functools.partial(local, pairs, cut),
        mesh=mesh,
        in_specs=(cube,) * 6 + (sheet, sheet),
        out_specs=(cube, cube),
        check_vma=False,
    )
```

```python
import functools

import jax
import jax.numpy as jnp
from jax import lax
from jax.experimental import pallas as pl
from jax.experimental.pallas import tpu as pltpu
from jax.sharding import PartitionSpec as P

thermal_coef = 0.1655
haline_coef = 0.76554
thermal_curve = 0.05952
haline_curve = 0.00054914
thermal_press = 0.0001497
haline_press = 1.109e-05
cabbeling = 0.0024341
bottom_depth = 5800.0
slope_limit = 1.0
strat_offset = 0.1

ROWS = 8
LANES = 128
GRID_AXES = ("gy", "gx")


def padded(levels):
    return -(-(levels + 2) // 8) * 8


def density(temper, saline, strata_height):
    heat_slope = -thermal_coef * (1.0 + thermal_press * strata_height)
    salt_slope = haline_coef * (1.0 - haline_press * strata_height)
    return (
        heat_slope - (0.5 * thermal_coef * thermal_curve) * temper - cabbeling * saline
    ) * temper + (salt_slope - (0.5 * haline_coef * haline_curve) * saline) * saline


def quotient(top, bottom):
    return top / bottom


def face_flux(speed, half_diffus, wet, left, right):
    steps = jnp.maximum(left[5] + right[5], 0.0) + 4.0 * strat_offset
    quarter = jnp.clip(quotient(right[2] - left[2], steps), -0.25 * slope_limit, 0.25 * slope_limit)
    forward = speed > 0.0

    def one(i):
        carried = speed * jnp.where(forward, left[i], right[i])
        mixed = half_diffus * (right[i] - left[i] - quarter * (left[3 + i] + right[3 + i]))
        return jnp.where(wet, carried - mixed, 0.0)

    return one(0), one(1)


def fetch(sources, targets, sems):
    copies = [pltpu.make_async_copy(a, b, sems.at[i]) for i, (a, b) in enumerate(zip(sources, targets))]
    for copy in copies:
        copy.start()
    return copies


def pack_kernel(
    levels, t_hbm, s_hbm, v_hbm, u_hbm, diff_hbm, depth_hbm,
    b_ref, xb_ref, xa_ref, a_ref, own_xa_ref, own_xb_ref, first_ref, t_ref, s_ref, v_ref, u_ref, diff_ref, depth_ref, sems,
):
    copies = fetch(
        (t_hbm, s_hbm, v_hbm, u_hbm, diff_hbm, depth_hbm),
        [ref.at[pl.ds(0, levels)] for ref in (t_ref, s_ref, v_ref, u_ref)] + [diff_ref, depth_ref],
        sems,
    )
    block = padded(levels)
    gy, gx = lax.axis_index("gy"), lax.axis_index("gx")
    y_even, x_even = gy % 2 == 0, gx % 2 == 0
    is_top = gy == lax.axis_size("gy") - 1
    lane = lax.broadcasted_iota(jnp.int32, (block, LANES), 1)
    source = jnp.where(is_top, LANES - 1 - lane, lane)
    one_lane = lax.broadcasted_iota(jnp.int32, (ROWS, LANES), 1)
    copies[4].wait()
    copies[5].wait()
    depth = depth_ref[...].astype(jnp.float32)
    diff = diff_ref[...]
    for ref in (t_ref, s_ref, v_ref, u_ref):
        ref[levels:] = jnp.zeros((block - levels, ROWS, LANES), jnp.float32)
    index = lax.broadcasted_iota(jnp.int32, (block, LANES), 0)

    def row_part(ref, i):
        ref = ref.reshape(block * ROWS, LANES)
        top = ref[pl.ds(ROWS - 1, block, stride=ROWS), :]
        low = ref[pl.ds(0, block, stride=ROWS), :]
        near, far = jnp.where(y_even, top, low), jnp.where(y_even, low, top)
        if i == 0:
            for name, value in ((levels, diff), (levels + 1, depth)):
                near = jnp.where(index == name, jnp.where(y_even, value[ROWS - 1 :], value[:1]), near)
                far = jnp.where(index == name, jnp.where(y_even, value[:1], value[ROWS - 1 :]), far)
        b_ref[i * block : (i + 1) * block] = jnp.take_along_axis(far, source, axis=1, mode="promise_in_bounds")
        if i < 2:
            a_ref[i * block : (i + 1) * block] = near
        else:
            whole = levels // ROWS * ROWS
            a_ref[2 * block :] = near[:whole]
            a_ref[block - (levels - whole) : block] = near[whole:levels]

    def column_part(ref, i):
        planes = [ref[k] for k in range(levels)]
        if i == 0:
            planes += [diff, depth]
        zero = jnp.zeros((ROWS, LANES), jnp.float32)
        east, west = [zero] * 4, [zero] * 4
        for k, plane in enumerate(planes):
            moved = pltpu.roll(plane, k + 1, 1)
            east[k % 4] = jnp.where(one_lane == k, moved, east[k % 4])
            if i < 2:
                west[k % 4] = jnp.where(one_lane == k + 1, moved, west[k % 4])
        east = (east[0] + east[1]) + (east[2] + east[3])
        west = (west[0] + west[1]) + (west[2] + west[3])
        part = slice(i * ROWS, (i + 1) * ROWS)
        own_xa_ref[part] = jnp.where(x_even, east, west)
        own_xb_ref[part] = jnp.where(x_even, west, east)
        east, west = pltpu.roll(east, 1, 1), pltpu.roll(west, LANES - 1, 1)
        xa, xb = jnp.where(x_even, east, west), jnp.where(x_even, west, east)
        xa_ref[part] = xa
        xb_ref[part] = xb
        first_ref[part] = jnp.where(below_middle(gy), xb, xa)

    copies[0].wait()
    copies[1].wait()
    for i, ref in enumerate((t_ref, s_ref)):
        row_part(ref, i)
        column_part(ref, i)
    copies[2].wait()
    copies[3].wait()
    row_part(v_ref, 2)
    column_part(u_ref, 2)


def below_middle(gy):
    return gy == lax.axis_size("gy") // 2 - 1


def starts_early(gy, gx, cut):
    ny = lax.axis_size("gy")
    return jnp.logical_and(gy < ny // 2, gx % cut < cut // 2)


def early_kernel(levels, group, cut, *refs):
    @pl.when(starts_early(lax.axis_index("gy"), lax.axis_index("gx"), cut))
    def _():
        inner(levels, group, *refs)


def late_kernel(levels, group, cut, *refs):
    n_in, n_out = 10, 9
    ins, outs = refs[:n_in], refs[n_in + n_out :]

    @pl.when(jnp.logical_not(starts_early(lax.axis_index("gy"), lax.axis_index("gx"), cut)))
    def _():
        inner(levels, group, *ins, *outs)


def inner(
    levels, group, t_ref, s_ref, u_ref, v_ref, w_ref, kap_ref, diff_ref, depth_ref,
    own_xa_ref, own_xb_ref, star_t_ref, star_s_ref, inv_ref, low_ref, ratio_ref, own_a_ref, own_b_ref,
    side_xa_ref, side_xb_ref,
):
    block = padded(levels)
    depth = depth_ref[...]
    diff = diff_ref[...]
    lane = lax.broadcasted_iota(jnp.int32, (ROWS, LANES), 1)
    row = lax.broadcasted_iota(jnp.int32, (ROWS, LANES), 0)

    def east(x):
        return pltpu.roll(x, LANES - 1, 1)

    def west(x):
        return pltpu.roll(x, 1, 1)

    def north(x):
        return pltpu.roll(x, ROWS - 1, 0)

    def south(x):
        return pltpu.roll(x, 1, 0)

    depth_x = jnp.where(lane == LANES - 1, 0, jnp.minimum(depth, east(depth)))
    depth_y = jnp.where(row == ROWS - 1, 0, jnp.minimum(depth, north(depth)))
    diff_x = 0.5 * (diff + east(diff))
    diff_y = 0.5 * (diff + north(diff))

    def at(ref, k):
        return ref[k]

    def height(k):
        part = (k.astype(jnp.float32) + 0.5) / levels
        return bottom_depth * (part * part)

    def level(k, carry):
        t, s, dens, step_t, step_s, step_d, top_t, top_s = carry
        below = jnp.minimum(k + 1, levels - 1)
        open_below = k + 1 < depth
        t1, s1 = at(t_ref, below), at(s_ref, below)
        dens1 = density(t1, s1, height(below))
        next_t = jnp.where(open_below, t1 - t, 0.0)
        next_s = jnp.where(open_below, s1 - s, 0.0)
        next_d = jnp.where(open_below, dens1 - dens, 0.0)
        w1 = at(w_ref, below)
        up = w1 > 0.0
        low_t = jnp.where(open_below, w1 * jnp.where(up, t1, t), 0.0)
        low_s = jnp.where(open_below, w1 * jnp.where(up, s1, s), 0.0)
        here = (t, s, dens, step_t + next_t, step_s + next_s, step_d + next_d)
        fx_t, fx_s = face_flux(at(u_ref, k), diff_x, k < depth_x, here, tuple(map(east, here)))
        fy_t, fy_s = face_flux(at(v_ref, k), diff_y, k < depth_y, here, tuple(map(north, here)))
        star_t_ref[k] = t - (fx_t - west(fx_t)) - (fy_t - south(fy_t)) - (top_t - low_t)
        star_s_ref[k] = s - (fx_s - west(fx_s)) - (fy_s - south(fy_s)) - (top_s - low_s)
        return t1, s1, dens1, next_t, next_s, next_d, low_t, low_s

    zero = jnp.zeros((ROWS, LANES), jnp.float32)
    t0, s0 = t_ref[0], s_ref[0]
    first = (t0, s0, density(t0, s0, bottom_depth * (0.5 / levels) ** 2), zero, zero, zero, zero, zero)

    middle = levels // 2

    def coupling(k):
        return jnp.where(k < depth, kap_ref[k], 0.0)

    def eliminate(j, carry):
        above, ratio, below, ratio_up = carry
        k = j
        under = coupling(k + 1)
        inv = quotient(1.0, 1.0 + above + under - above * ratio)
        inv_ref[k] = inv
        low_ref[k] = above * inv
        ratio = under * inv
        ratio_ref[k] = ratio
        k = levels - 1 - j
        over = coupling(k)
        inv = quotient(1.0, 1.0 + over + below - below * ratio_up)
        inv_ref[k] = inv
        low_ref[k] = below * inv
        ratio_up = over * inv
        ratio_ref[k] = ratio_up
        return under, ratio, over, ratio_up

    rounds = levels // group
    pairs = min((middle // rounds, -(-middle // rounds)), key=lambda p: middle - min(rounds, middle // p) * p)
    whole = min(rounds, middle // pairs)

    def both(i, carry):
        one, two = carry
        for j in range(group):
            one = level(i * group + j, one)
            if j < pairs:
                two = eliminate(i * pairs + j, two)
        return one, two

    def some(i, carry):
        for j in range(group):
            carry = level(i * group + j, carry)
        return carry

    carry, elimination = lax.fori_loop(0, whole, both, (first, (zero, zero, zero, zero)))
    lax.fori_loop(whole, rounds, some, carry)
    for j in range(whole * pairs, middle):
        elimination = eliminate(jnp.int32(j), elimination)
    above, ratio, below, ratio_up = elimination
    inv = 1.0 / (1.0 + above + below - above * ratio - below * ratio_up)
    inv_ref[middle] = inv
    low_ref[middle] = above * inv
    ratio_ref[middle] = below * inv

    gy = lax.axis_index("gy")
    y_even = gy % 2 == 0
    depth_f = depth.astype(jnp.float32)
    index = lax.broadcasted_iota(jnp.int32, (block, LANES), 0)
    heights = level_heights(index, levels)
    flats = [ref.reshape(block * ROWS, LANES) for ref in (t_ref, s_ref, v_ref)]
    tops = [flat[pl.ds(ROWS - 1, block, stride=ROWS), :] for flat in flats]
    lows = [flat[pl.ds(0, block, stride=ROWS), :] for flat in flats]
    for own_ref, keep_top in ((own_a_ref, y_even), (own_b_ref, jnp.logical_not(y_even))):
        t, s, q = (jnp.where(keep_top, top, low) for top, low in zip(tops, lows))
        edge_diff, edge_depth = (
            jnp.where(keep_top, value[ROWS - 1 :], value[:1]) for value in (diff, depth_f)
        )
        for i, field in enumerate(side(t, s, edge_depth, index.astype(jnp.float32), heights, 0) + (q,)):
            if i == 0:
                field = jnp.where(index == levels, edge_diff, jnp.where(index == levels + 1, edge_depth, field))
            own_ref[i * block : (i + 1) * block] = field
    x_even = lax.axis_index("gx") % 2 == 0
    for own_ref, side_ref, own_left in ((own_xa_ref, side_xa_ref, x_even), (own_xb_ref, side_xb_ref, jnp.logical_not(x_even))):
        t, s, q = (own_ref[i * ROWS : (i + 1) * ROWS] for i in range(3))
        ahead = jnp.where(own_left, 0, 1)
        values = column_side(t, s, levels, ahead) + (q,) + edge_values(t, levels, ahead)
        for i, value in enumerate(values):
            side_ref[i * ROWS : (i + 1) * ROWS] = value


def level_heights(index, levels):
    part = (index.astype(jnp.float32) + 0.5) / levels
    return bottom_depth * (part * part)


def column_sums(x, open_here, axis):
    size = x.shape[axis]
    step = jnp.where(open_here, x - pltpu.roll(x, 1, axis), 0.0)
    return step + pltpu.roll(step, size - 1, axis)


def side(temper, saline, depth, index, heights, axis):
    dens = density(temper, saline, heights)
    open_here = jnp.logical_and(index >= 1, index < depth)
    return (
        temper,
        saline,
        dens,
        column_sums(temper, open_here, axis),
        column_sums(saline, open_here, axis),
        column_sums(dens, open_here, axis),
    )


def edge_values(t, levels, ahead):
    one, two, three = (t[:, levels + i : levels + i + 1] for i in range(3))
    first, second = jnp.where(ahead == 0, one, two), jnp.where(ahead == 0, two, three)
    return jnp.broadcast_to(first, t.shape), jnp.broadcast_to(second, t.shape)


def column_side(t, s, levels, ahead):
    depth = edge_values(t, levels, ahead)[1]
    level = lax.broadcasted_iota(jnp.int32, t.shape, 1) - ahead
    here, over, under = (
        (
            pltpu.roll(t, shift, 1) if shift else t,
            pltpu.roll(s, shift, 1) if shift else s,
            level_heights(level - move, levels),
        )
        for shift, move in ((0, 0), (1, 1), (LANES - 1, -1))
    )
    level = level.astype(jnp.float32)
    open_here = jnp.logical_and(level >= 1.0, level < depth)
    open_under = level + 1.0 < depth
    here, over, under = (x[:2] + (density(*x),) for x in (here, over, under))
    sums = tuple(
        jnp.where(open_here, h - o, 0.0) + jnp.where(open_under, u - h, 0.0) for h, o, u in zip(here, over, under)
    )
    return here + sums


def edge_change(own, got, own_speed, got_speed, diffus, wet, own_left, fold=None):
    sign = jnp.where(own_left, 1.0, -1.0)
    speed = jnp.where(own_left, own_speed, got_speed)
    if fold is not None:
        speed = jnp.where(fold, 0.5 * (own_speed - got_speed), speed)
    outward = sign * speed
    steps = jnp.maximum(own[5] + got[5], 0.0) + 4.0 * strat_offset
    quarter = jnp.clip(quotient(got[2] - own[2], steps), -0.25 * slope_limit, 0.25 * slope_limit)
    leaves = outward > 0.0

    def one(i):
        carried = outward * jnp.where(leaves, own[i], got[i])
        mixed = diffus * (got[i] - own[i] - quarter * (own[3 + i] + got[3 + i]))
        return jnp.where(wet, mixed - carried, 0.0)

    return one(0), one(1)


def final_kernel(
    levels, cut, got_first, got_b, got_relay, got_xb, got_xa, got_a, own_a, own_b, side_xa, side_xb, _,
    star_t_ref, star_s_ref, inv_ref, low_ref, ratio_ref,
    out_t_ref, out_s_ref, change_ref,
):
    block = padded(levels)
    gy, gx = lax.axis_index("gy"), lax.axis_index("gx")
    y_even, x_even = gy % 2 == 0, gx % 2 == 0
    y_odd, x_odd = jnp.logical_not(y_even), jnp.logical_not(x_even)
    is_top = gy == lax.axis_size("gy") - 1
    corner = jnp.logical_and(is_far_row(gy), is_far_column(gx, cut))
    xb_first = jnp.logical_and(below_middle(gy), gx % cut < 3)
    xa_first = jnp.logical_and(starts_early(gy, gx, cut), jnp.logical_not(below_middle(gy)))

    index = lax.broadcasted_iota(jnp.int32, (block, LANES), 0)
    height = level_heights(index, levels)
    level = index.astype(jnp.float32)

    def row_change(place, own_ref, t, s, q, own_left, fold):
        own = [own_ref[i * block : (i + 1) * block] for i in range(7)]
        diffus, depth = t[levels : levels + 1], t[levels + 1 : levels + 2]
        own_diffus, own_depth = own[0][levels : levels + 1], own[0][levels + 1 : levels + 2]
        changes = edge_change(
            own, side(t, s, depth, level, height, 0), own[6], q,
            0.5 * (own_diffus + diffus), level < jnp.minimum(own_depth, depth), own_left, fold,
        )
        for i in range(2):
            change_ref[place, i] = changes[i]

    whole = levels // ROWS * ROWS
    t, s = got_a[:block], got_a[block : 2 * block]
    q = jnp.concatenate(
        [got_a[2 * block :], t[block - (levels - whole) :], jnp.zeros((block - levels, LANES), jnp.float32)], 0
    )
    row_change(0, own_a, t, s, q, y_even, None)
    row_change(1, own_b, *(got_b[i * block : (i + 1) * block] for i in range(3)), y_odd, is_top)

    lane = lax.broadcasted_iota(jnp.int32, (ROWS, LANES), 1)
    row = lax.broadcasted_iota(jnp.int32, (ROWS, LANES), 0)

    def column_change(side_ref, got, own_left):
        own = [side_ref[i * ROWS : (i + 1) * ROWS] for i in range(9)]
        ahead = jnp.where(own_left, 0, 1)
        diffus, depth = edge_values(got[0], levels, ahead)
        level = (lane - ahead).astype(jnp.float32)
        wet = jnp.logical_and(level >= 0.0, level < jnp.minimum(own[8], depth))
        return edge_change(
            own, column_side(got[0], got[1], levels, ahead), own[6], got[2], 0.5 * (own[7] + diffus), wet, own_left
        )

    def thirds(ref):
        return [ref[i * ROWS : (i + 1) * ROWS] for i in range(3)]

    first, relay = thirds(got_first), thirds(got_relay)
    from_xa = [jnp.where(xa_first, a, b) for a, b in zip(first, thirds(got_xa))]
    from_xb = [
        jnp.where(xb_first, a, jnp.where(corner, b, c)) for a, b, c in zip(first, relay, thirds(got_xb))
    ]
    change_xa = column_change(side_xa, from_xa, x_even)
    change_xb = column_change(side_xb, from_xb, x_odd)
    even_lane = lane % 2 == 0
    paired = []
    for i in range(2):
        last = jnp.where(x_even, change_xa[i], change_xb[i])
        first = jnp.where(x_even, change_xb[i], change_xa[i])
        paired.append((jnp.where(even_lane, last, first), jnp.where(even_lane, first, last)))
    at_side = jnp.logical_or(lane == 0, lane == LANES - 1)
    row_a = row == jnp.where(y_even, ROWS - 1, 0)
    row_b = row == jnp.where(y_even, 0, ROWS - 1)

    def right_side(i, k):
        ref = (star_t_ref, star_s_ref)[i]
        x_part = jnp.where(at_side, pltpu.roll(paired[i][k % 2], (LANES - 1 - k) % LANES, 1), 0.0)
        y_part = jnp.where(
            row_a, change_ref[0, i, k : k + 1, :], jnp.where(row_b, change_ref[1, i, k : k + 1, :], 0.0)
        )
        return (ref[k] + (x_part + y_part)) * inv_ref[k]

    outs = (out_t_ref, out_s_ref)
    middle = levels // 2
    zero = jnp.zeros((ROWS, LANES), jnp.float32)
    upper, lower = [zero, zero], [zero, zero]
    for j in range(middle):
        for i in range(2):
            upper[i] = right_side(i, j) + low_ref[j] * upper[i]
            outs[i][j] = upper[i]
            k = levels - 1 - j
            lower[i] = right_side(i, k) + low_ref[k] * lower[i]
            outs[i][k] = lower[i]
    for i in range(2):
        solved = right_side(i, middle) + low_ref[middle] * upper[i] + ratio_ref[middle] * lower[i]
        outs[i][middle] = solved
        upper[i] = lower[i] = solved
    for j in range(1, middle + 1):
        for i in range(2):
            k = middle - j
            upper[i] = outs[i][k] + ratio_ref[k] * upper[i]
            outs[i][k] = upper[i]
            k = middle + j
            lower[i] = outs[i][k] + ratio_ref[k] * lower[i]
            outs[i][k] = lower[i]


def call(kernel, outs, operands, memory, scratch=(), flops=0, name=None, aliases=None):
    return pl.pallas_call(
        kernel,
        out_shape=[jax.ShapeDtypeStruct(getattr(s, "shape", s), getattr(s, "dtype", jnp.float32)) for s in outs],
        in_specs=[pl.BlockSpec(memory_space=memory)] * len(operands),
        out_specs=[pl.BlockSpec(memory_space=pltpu.VMEM)] * len(outs),
        scratch_shapes=list(scratch),
        input_output_aliases=aliases or {},
        compiler_params=pltpu.CompilerParams(vmem_limit_bytes=24 * 1024 * 1024),
        cost_estimate=pl.CostEstimate(flops=flops, bytes_accessed=4 * 1024 * 1024, transcendentals=0),
        name=name,
    )(*operands)


def local(pairs, cut, heat, salt, u, v, w, kap, diff, depth):
    levels, rows, lanes = heat.shape
    block = padded(levels)
    cube, wide, thin = (levels, rows, lanes), (3 * block, lanes), (3 * rows, lanes)
    compact = (2 * block + levels // rows * rows, lanes)

    def moved(x, which):
        return lax.ppermute(x, GRID_AXES, pairs[which])

    operands = tuple(pltpu.with_memory_space_constraint(x, pltpu.HBM) for x in (heat, salt, v, u, diff, depth))
    pack_b, pack_xb, pack_xa, pack_a, own_xa, own_xb, pack_first, heat, salt, v, u, diff, depth = call(
        functools.partial(pack_kernel, levels), [wide, thin, thin, compact, thin, thin, thin] + [(block, rows, lanes)] * 4 + [diff.shape, depth],
        operands, pltpu.HBM, [pltpu.SemaphoreType.DMA((6,))], name="pack",
    )
    group = next(g for g in (15, 5, 3, 2, 1) if levels % g == 0)
    operands = (heat, salt, u, v, w, kap, diff, depth, own_xa, own_xb)
    results = [cube] * 5 + [(7 * block, lanes)] * 2 + [(9 * rows, lanes)] * 2
    early = list(
        call(functools.partial(early_kernel, levels, group, cut), results, operands, pltpu.VMEM, name="early")
    )
    got_first = moved(pack_first, "first")
    pack_b, early[0] = lax.optimization_barrier((pack_b, early[0]))
    got_b = moved(pack_b, "b")
    relayed = moved(pack_xb, "relay")
    got_xb = moved(pack_xb, "xb")
    got_xa = moved(pack_xa, "xa")
    got_a = moved(pack_a, "a")
    got_first, early[0] = lax.optimization_barrier((got_first, early[0]))
    star_t, star_s, inv, low, ratio, own_a, own_b, side_xa, side_xb = call(
        functools.partial(late_kernel, levels, group, cut), results, operands + tuple(early), pltpu.VMEM,
        flops=1_145_000_000, name="late", aliases={10 + i: i for i in range(9)},
    )
    relayed, star_t = lax.optimization_barrier((relayed, star_t))
    got_relay = moved(relayed, "hand_on")
    operands = (
        got_first, got_b, got_relay, got_xb, got_xa, got_a, own_a, own_b, side_xa, side_xb, pack_xa,
        star_t, star_s, inv, low, ratio,
    )
    return call(
        functools.partial(final_kernel, levels, cut),
        [cube] * 2, operands, pltpu.VMEM, [pltpu.VMEM((2, 2, block, lanes), jnp.float32)], name="final",
    )


def is_far_row(y):
    ny = lax.axis_size("gy")
    return (y == ny // 2 - 1) | (y == ny // 2) | (y == ny - 1)


def is_far_column(x, cut):
    return (x % cut == 0) | (x % cut == cut - 1)


def solution(mesh):
    ny, nx = mesh.shape["gy"], mesh.shape["gx"]
    cut = nx // 4
    far_rows = (ny // 2 - 1, ny // 2, ny - 1)
    far_columns = [x for x in range(nx) if x % cut in (0, cut - 1)]

    def at(y, x):
        return y * nx + x

    def beside(x):
        return (((x + 1) ^ 1) - 1) % nx

    second = [(y, ((y + 1) ^ 1) - 1, x, x) for y in range(1, ny - 1) for x in range(nx)]
    second += [(ny - 1, ny - 1, x, nx - 1 - x) for x in range(nx)]
    corners = [(y, x) for y in far_rows for x in far_columns]
    pairs = {
        "a": [(at(y, x), at(y ^ 1, x)) for y in range(ny) for x in range(nx)],
        "b": [(at(y, x), at(to_y, to_x)) for y, to_y, x, to_x in second],
        "first": [(at(y, x), at(y, x ^ 1)) for y in range(ny // 2 - 1) for x in range(nx) if x % cut < cut // 2]
        + [(at(y, x), at(y, beside(x))) for y in (ny // 2 - 1,) for x in range(nx) if x % cut in (1, 2, cut - 1)],
        "xa": [(at(y, x), at(y, x ^ 1)) for y in range(ny) for x in range(nx) if y >= ny // 2 - 1 or x % cut >= cut // 2],
        "xb": [(at(y, x), at(y, beside(x))) for y in range(ny) for x in range(nx) if (y, x) not in corners and (y != ny // 2 - 1 or x % cut > 2)],
        "relay": [(at(y, x), at(y ^ 1, beside(x))) for y, x in corners if y >= ny // 2 or x % cut == 0],
        "hand_on": [(at(y ^ 1, x), at(y, x)) for y, x in corners if y >= ny // 2 or x % cut == cut - 1],
    }
    cube = P(None, "gy", "gx")
    sheet = P("gy", "gx")
    return jax.shard_map(
        functools.partial(local, pairs, cut),
        mesh=mesh,
        in_specs=(cube,) * 6 + (sheet, sheet),
        out_specs=(cube, cube),
        check_vma=False,
    )
```

```python
import functools

import jax
import jax.numpy as jnp
from jax import lax
from jax.experimental import pallas as pl
from jax.experimental.pallas import tpu as pltpu
from jax.sharding import PartitionSpec as P

thermal_coef = 0.1655
haline_coef = 0.76554
thermal_curve = 0.05952
haline_curve = 0.00054914
thermal_press = 0.0001497
haline_press = 1.109e-05
cabbeling = 0.0024341
bottom_depth = 5800.0
slope_limit = 1.0
strat_offset = 0.1

ROWS = 8
LANES = 128
GRID_AXES = ("gy", "gx")


def padded(levels):
    return -(-(levels + 2) // 8) * 8


def density(temper, saline, strata_height):
    heat_slope = -thermal_coef * (1.0 + thermal_press * strata_height)
    salt_slope = haline_coef * (1.0 - haline_press * strata_height)
    return (
        heat_slope - (0.5 * thermal_coef * thermal_curve) * temper - cabbeling * saline
    ) * temper + (salt_slope - (0.5 * haline_coef * haline_curve) * saline) * saline


def quotient(top, bottom):
    return top / bottom


def face_flux(speed, half_diffus, wet, left, right):
    steps = jnp.maximum(left[5] + right[5], 0.0) + 4.0 * strat_offset
    quarter = jnp.clip(quotient(right[2] - left[2], steps), -0.25 * slope_limit, 0.25 * slope_limit)
    forward = speed > 0.0

    def one(i):
        carried = speed * jnp.where(forward, left[i], right[i])
        mixed = half_diffus * (right[i] - left[i] - quarter * (left[3 + i] + right[3 + i]))
        return jnp.where(wet, carried - mixed, 0.0)

    return one(0), one(1)


def fetch(sources, targets, sems):
    copies = [pltpu.make_async_copy(a, b, sems.at[i]) for i, (a, b) in enumerate(zip(sources, targets))]
    for copy in copies:
        copy.start()
    return copies


def pack_kernel(
    levels, cut, t_hbm, s_hbm, v_hbm, u_hbm, diff_hbm, depth_hbm,
    b_ref, xb_ref, xa_ref, a_ref, own_xa_ref, own_xb_ref, first_ref, second_ref, t_ref, s_ref, v_ref, u_ref, diff_ref, depth_ref, sems,
):
    copies = fetch(
        (t_hbm, s_hbm, v_hbm, u_hbm, diff_hbm, depth_hbm),
        [ref.at[pl.ds(0, levels)] for ref in (t_ref, s_ref, v_ref, u_ref)] + [diff_ref, depth_ref],
        sems,
    )
    block = padded(levels)
    gy, gx = lax.axis_index("gy"), lax.axis_index("gx")
    y_even, x_even = gy % 2 == 0, gx % 2 == 0
    is_top = gy == lax.axis_size("gy") - 1
    lane = lax.broadcasted_iota(jnp.int32, (block, LANES), 1)
    source = jnp.where(is_top, LANES - 1 - lane, lane)
    one_lane = lax.broadcasted_iota(jnp.int32, (ROWS, LANES), 1)
    copies[4].wait()
    copies[5].wait()
    depth = depth_ref[...].astype(jnp.float32)
    diff = diff_ref[...]
    for ref in (t_ref, s_ref, v_ref, u_ref):
        ref[levels:] = jnp.zeros((block - levels, ROWS, LANES), jnp.float32)
    index = lax.broadcasted_iota(jnp.int32, (block, LANES), 0)

    def row_part(ref, i):
        ref = ref.reshape(block * ROWS, LANES)
        top = ref[pl.ds(ROWS - 1, block, stride=ROWS), :]
        low = ref[pl.ds(0, block, stride=ROWS), :]
        near, far = jnp.where(y_even, top, low), jnp.where(y_even, low, top)
        if i == 0:
            for name, value in ((levels, diff), (levels + 1, depth)):
                near = jnp.where(index == name, jnp.where(y_even, value[ROWS - 1 :], value[:1]), near)
                far = jnp.where(index == name, jnp.where(y_even, value[:1], value[ROWS - 1 :]), far)
        b_ref[i * block : (i + 1) * block] = jnp.take_along_axis(far, source, axis=1, mode="promise_in_bounds")
        if i < 2:
            a_ref[i * block : (i + 1) * block] = near
        else:
            whole = levels // ROWS * ROWS
            a_ref[2 * block :] = near[:whole]
            a_ref[block - (levels - whole) : block] = near[whole:levels]

    def column_part(ref, i):
        planes = [ref[k] for k in range(levels)]
        if i == 0:
            planes += [diff, depth]
        zero = jnp.zeros((ROWS, LANES), jnp.float32)
        east, west = [zero] * 4, [zero] * 4
        for k, plane in enumerate(planes):
            moved = pltpu.roll(plane, k + 1, 1)
            east[k % 4] = jnp.where(one_lane == k, moved, east[k % 4])
            if i < 2:
                west[k % 4] = jnp.where(one_lane == k + 1, moved, west[k % 4])
        east = (east[0] + east[1]) + (east[2] + east[3])
        west = (west[0] + west[1]) + (west[2] + west[3])
        part = slice(i * ROWS, (i + 1) * ROWS)
        own_xa_ref[part] = jnp.where(x_even, east, west)
        own_xb_ref[part] = jnp.where(x_even, west, east)
        east, west = pltpu.roll(east, 1, 1), pltpu.roll(west, LANES - 1, 1)
        xa, xb = jnp.where(x_even, east, west), jnp.where(x_even, west, east)
        xa_ref[part] = xa
        xb_ref[part] = xb
        first_ref[part] = jnp.where(below_middle(gy), xb, xa)
        second_ref[part] = jnp.where(jnp.logical_and(below_middle(gy), gx % cut < 2), xa, xb)

    copies[0].wait()
    copies[1].wait()
    for i, ref in enumerate((t_ref, s_ref)):
        row_part(ref, i)
        column_part(ref, i)
    copies[2].wait()
    copies[3].wait()
    row_part(v_ref, 2)
    column_part(u_ref, 2)


def below_middle(gy):
    return gy == lax.axis_size("gy") // 2 - 1


def starts_early(gy, gx, cut):
    ny = lax.axis_size("gy")
    return jnp.logical_and(gy < ny // 2, gx % cut < cut // 2)


def early_kernel(levels, group, cut, *refs):
    @pl.when(starts_early(lax.axis_index("gy"), lax.axis_index("gx"), cut))
    def _():
        inner(levels, group, *refs)


def late_kernel(levels, group, cut, *refs):
    n_in, n_out = 10, 9
    ins, outs = refs[:n_in], refs[n_in + n_out :]

    @pl.when(jnp.logical_not(starts_early(lax.axis_index("gy"), lax.axis_index("gx"), cut)))
    def _():
        inner(levels, group, *ins, *outs)


def inner(
    levels, group, t_ref, s_ref, u_ref, v_ref, w_ref, kap_ref, diff_ref, depth_ref,
    own_xa_ref, own_xb_ref, star_t_ref, star_s_ref, inv_ref, low_ref, ratio_ref, own_a_ref, own_b_ref,
    side_xa_ref, side_xb_ref,
):
    block = padded(levels)
    depth = depth_ref[...]
    diff = diff_ref[...]
    lane = lax.broadcasted_iota(jnp.int32, (ROWS, LANES), 1)
    row = lax.broadcasted_iota(jnp.int32, (ROWS, LANES), 0)

    def east(x):
        return pltpu.roll(x, LANES - 1, 1)

    def west(x):
        return pltpu.roll(x, 1, 1)

    def north(x):
        return pltpu.roll(x, ROWS - 1, 0)

    def south(x):
        return pltpu.roll(x, 1, 0)

    depth_x = jnp.where(lane == LANES - 1, 0, jnp.minimum(depth, east(depth)))
    depth_y = jnp.where(row == ROWS - 1, 0, jnp.minimum(depth, north(depth)))
    diff_x = 0.5 * (diff + east(diff))
    diff_y = 0.5 * (diff + north(diff))

    def at(ref, k):
        return ref[k]

    def height(k):
        part = (k.astype(jnp.float32) + 0.5) / levels
        return bottom_depth * (part * part)

    def level(k, carry):
        t, s, dens, step_t, step_s, step_d, top_t, top_s = carry
        below = jnp.minimum(k + 1, levels - 1)
        open_below = k + 1 < depth
        t1, s1 = at(t_ref, below), at(s_ref, below)
        dens1 = density(t1, s1, height(below))
        next_t = jnp.where(open_below, t1 - t, 0.0)
        next_s = jnp.where(open_below, s1 - s, 0.0)
        next_d = jnp.where(open_below, dens1 - dens, 0.0)
        w1 = at(w_ref, below)
        up = w1 > 0.0
        low_t = jnp.where(open_below, w1 * jnp.where(up, t1, t), 0.0)
        low_s = jnp.where(open_below, w1 * jnp.where(up, s1, s), 0.0)
        here = (t, s, dens, step_t + next_t, step_s + next_s, step_d + next_d)
        fx_t, fx_s = face_flux(at(u_ref, k), diff_x, k < depth_x, here, tuple(map(east, here)))
        fy_t, fy_s = face_flux(at(v_ref, k), diff_y, k < depth_y, here, tuple(map(north, here)))
        star_t_ref[k] = t - (fx_t - west(fx_t)) - (fy_t - south(fy_t)) - (top_t - low_t)
        star_s_ref[k] = s - (fx_s - west(fx_s)) - (fy_s - south(fy_s)) - (top_s - low_s)
        return t1, s1, dens1, next_t, next_s, next_d, low_t, low_s

    zero = jnp.zeros((ROWS, LANES), jnp.float32)
    t0, s0 = t_ref[0], s_ref[0]
    first = (t0, s0, density(t0, s0, bottom_depth * (0.5 / levels) ** 2), zero, zero, zero, zero, zero)

    middle = levels // 2

    def coupling(k):
        return jnp.where(k < depth, kap_ref[k], 0.0)

    def eliminate(j, carry):
        above, ratio, below, ratio_up = carry
        k = j
        under = coupling(k + 1)
        inv = quotient(1.0, 1.0 + above + under - above * ratio)
        inv_ref[k] = inv
        low_ref[k] = above * inv
        ratio = under * inv
        ratio_ref[k] = ratio
        k = levels - 1 - j
        over = coupling(k)
        inv = quotient(1.0, 1.0 + over + below - below * ratio_up)
        inv_ref[k] = inv
        low_ref[k] = below * inv
        ratio_up = over * inv
        ratio_ref[k] = ratio_up
        return under, ratio, over, ratio_up

    rounds = levels // group
    pairs = min((middle // rounds, -(-middle // rounds)), key=lambda p: middle - min(rounds, middle // p) * p)
    whole = min(rounds, middle // pairs)

    def both(i, carry):
        one, two = carry
        for j in range(group):
            one = level(i * group + j, one)
            if j < pairs:
                two = eliminate(i * pairs + j, two)
        return one, two

    def some(i, carry):
        for j in range(group):
            carry = level(i * group + j, carry)
        return carry

    carry, elimination = lax.fori_loop(0, whole, both, (first, (zero, zero, zero, zero)))
    lax.fori_loop(whole, rounds, some, carry)
    for j in range(whole * pairs, middle):
        elimination = eliminate(jnp.int32(j), elimination)
    above, ratio, below, ratio_up = elimination
    inv = 1.0 / (1.0 + above + below - above * ratio - below * ratio_up)
    inv_ref[middle] = inv
    low_ref[middle] = above * inv
    ratio_ref[middle] = below * inv

    gy = lax.axis_index("gy")
    y_even = gy % 2 == 0
    depth_f = depth.astype(jnp.float32)
    index = lax.broadcasted_iota(jnp.int32, (block, LANES), 0)
    heights = level_heights(index, levels)
    flats = [ref.reshape(block * ROWS, LANES) for ref in (t_ref, s_ref, v_ref)]
    tops = [flat[pl.ds(ROWS - 1, block, stride=ROWS), :] for flat in flats]
    lows = [flat[pl.ds(0, block, stride=ROWS), :] for flat in flats]
    for own_ref, keep_top in ((own_a_ref, y_even), (own_b_ref, jnp.logical_not(y_even))):
        t, s, q = (jnp.where(keep_top, top, low) for top, low in zip(tops, lows))
        edge_diff, edge_depth = (
            jnp.where(keep_top, value[ROWS - 1 :], value[:1]) for value in (diff, depth_f)
        )
        for i, field in enumerate(side(t, s, edge_depth, index.astype(jnp.float32), heights, 0) + (q,)):
            if i == 0:
                field = jnp.where(index == levels, edge_diff, jnp.where(index == levels + 1, edge_depth, field))
            own_ref[i * block : (i + 1) * block] = field
    x_even = lax.axis_index("gx") % 2 == 0
    for own_ref, side_ref, own_left in ((own_xa_ref, side_xa_ref, x_even), (own_xb_ref, side_xb_ref, jnp.logical_not(x_even))):
        t, s, q = (own_ref[i * ROWS : (i + 1) * ROWS] for i in range(3))
        ahead = jnp.where(own_left, 0, 1)
        values = column_side(t, s, levels, ahead) + (q,) + edge_values(t, levels, ahead)
        for i, value in enumerate(values):
            side_ref[i * ROWS : (i + 1) * ROWS] = value


def level_heights(index, levels):
    part = (index.astype(jnp.float32) + 0.5) / levels
    return bottom_depth * (part * part)


def column_sums(x, open_here, axis):
    size = x.shape[axis]
    step = jnp.where(open_here, x - pltpu.roll(x, 1, axis), 0.0)
    return step + pltpu.roll(step, size - 1, axis)


def side(temper, saline, depth, index, heights, axis):
    dens = density(temper, saline, heights)
    open_here = jnp.logical_and(index >= 1, index < depth)
    return (
        temper,
        saline,
        dens,
        column_sums(temper, open_here, axis),
        column_sums(saline, open_here, axis),
        column_sums(dens, open_here, axis),
    )


def edge_values(t, levels, ahead):
    one, two, three = (t[:, levels + i : levels + i + 1] for i in range(3))
    first, second = jnp.where(ahead == 0, one, two), jnp.where(ahead == 0, two, three)
    return jnp.broadcast_to(first, t.shape), jnp.broadcast_to(second, t.shape)


def column_side(t, s, levels, ahead):
    depth = edge_values(t, levels, ahead)[1]
    level = lax.broadcasted_iota(jnp.int32, t.shape, 1) - ahead
    here, over, under = (
        (
            pltpu.roll(t, shift, 1) if shift else t,
            pltpu.roll(s, shift, 1) if shift else s,
            level_heights(level - move, levels),
        )
        for shift, move in ((0, 0), (1, 1), (LANES - 1, -1))
    )
    level = level.astype(jnp.float32)
    open_here = jnp.logical_and(level >= 1.0, level < depth)
    open_under = level + 1.0 < depth
    here, over, under = (x[:2] + (density(*x),) for x in (here, over, under))
    sums = tuple(
        jnp.where(open_here, h - o, 0.0) + jnp.where(open_under, u - h, 0.0) for h, o, u in zip(here, over, under)
    )
    return here + sums


def edge_change(own, got, own_speed, got_speed, diffus, wet, own_left, fold=None):
    sign = jnp.where(own_left, 1.0, -1.0)
    speed = jnp.where(own_left, own_speed, got_speed)
    if fold is not None:
        speed = jnp.where(fold, 0.5 * (own_speed - got_speed), speed)
    outward = sign * speed
    steps = jnp.maximum(own[5] + got[5], 0.0) + 4.0 * strat_offset
    quarter = jnp.clip(quotient(got[2] - own[2], steps), -0.25 * slope_limit, 0.25 * slope_limit)
    leaves = outward > 0.0

    def one(i):
        carried = outward * jnp.where(leaves, own[i], got[i])
        mixed = diffus * (got[i] - own[i] - quarter * (own[3 + i] + got[3 + i]))
        return jnp.where(wet, mixed - carried, 0.0)

    return one(0), one(1)


def columns_kernel(levels, cut, got_first, got_relay, got_xb, got_xa, side_xa, side_xb, pair_ref):
    gy, gx = lax.axis_index("gy"), lax.axis_index("gx")
    x_even = gx % 2 == 0
    x_odd = jnp.logical_not(x_even)
    corner = jnp.logical_and(is_far_row(gy), is_far_column(gx, cut))
    xb_first = jnp.logical_and(below_middle(gy), gx % cut < 3)
    xa_first = jnp.logical_and(starts_early(gy, gx, cut), jnp.logical_not(below_middle(gy)))

    lane = lax.broadcasted_iota(jnp.int32, (ROWS, LANES), 1)

    def column_change(side_ref, got, own_left):
        own = [side_ref[i * ROWS : (i + 1) * ROWS] for i in range(9)]
        ahead = jnp.where(own_left, 0, 1)
        diffus, depth = edge_values(got[0], levels, ahead)
        level = (lane - ahead).astype(jnp.float32)
        wet = jnp.logical_and(level >= 0.0, level < jnp.minimum(own[8], depth))
        return edge_change(
            own, column_side(got[0], got[1], levels, ahead), own[6], got[2], 0.5 * (own[7] + diffus), wet, own_left
        )

    def thirds(ref):
        return [ref[i * ROWS : (i + 1) * ROWS] for i in range(3)]

    first, relay = thirds(got_first), thirds(got_relay)
    xa_second = jnp.logical_and(below_middle(gy), gx % cut < 2)
    from_xa = [
        jnp.where(xa_first, a, jnp.where(xa_second, b, c))
        for a, b, c in zip(first, thirds(got_xb), thirds(got_xa))
    ]
    from_xb = [
        jnp.where(xb_first, a, jnp.where(corner, b, c)) for a, b, c in zip(first, relay, thirds(got_xb))
    ]
    change_xa = column_change(side_xa, from_xa, x_even)
    change_xb = column_change(side_xb, from_xb, x_odd)
    even_lane = lane % 2 == 0
    for i in range(2):
        last = jnp.where(x_even, change_xa[i], change_xb[i])
        first = jnp.where(x_even, change_xb[i], change_xa[i])
        pair_ref[i, 0] = jnp.where(even_lane, last, first)
        pair_ref[i, 1] = jnp.where(even_lane, first, last)


def final_kernel(
    levels, got_b, got_a, own_a, own_b, pair_ref,
    star_t_ref, star_s_ref, inv_ref, low_ref, ratio_ref,
    out_t_ref, out_s_ref, change_ref,
):
    block = padded(levels)
    gy = lax.axis_index("gy")
    y_even = gy % 2 == 0
    y_odd = jnp.logical_not(y_even)
    is_top = gy == lax.axis_size("gy") - 1
    index = lax.broadcasted_iota(jnp.int32, (block, LANES), 0)
    height = level_heights(index, levels)
    level = index.astype(jnp.float32)

    def row_change(place, own_ref, t, s, q, own_left, fold):
        own = [own_ref[i * block : (i + 1) * block] for i in range(7)]
        diffus, depth = t[levels : levels + 1], t[levels + 1 : levels + 2]
        own_diffus, own_depth = own[0][levels : levels + 1], own[0][levels + 1 : levels + 2]
        changes = edge_change(
            own, side(t, s, depth, level, height, 0), own[6], q,
            0.5 * (own_diffus + diffus), level < jnp.minimum(own_depth, depth), own_left, fold,
        )
        for i in range(2):
            change_ref[place, i] = changes[i]

    whole = levels // ROWS * ROWS
    t, s = got_a[:block], got_a[block : 2 * block]
    q = jnp.concatenate(
        [got_a[2 * block :], t[block - (levels - whole) :], jnp.zeros((block - levels, LANES), jnp.float32)], 0
    )
    row_change(0, own_a, t, s, q, y_even, None)
    row_change(1, own_b, *(got_b[i * block : (i + 1) * block] for i in range(3)), y_odd, is_top)

    lane = lax.broadcasted_iota(jnp.int32, (ROWS, LANES), 1)
    row = lax.broadcasted_iota(jnp.int32, (ROWS, LANES), 0)
    at_side = jnp.logical_or(lane == 0, lane == LANES - 1)
    row_a = row == jnp.where(y_even, ROWS - 1, 0)
    row_b = row == jnp.where(y_even, 0, ROWS - 1)

    def right_side(i, k):
        ref = (star_t_ref, star_s_ref)[i]
        x_part = jnp.where(at_side, pltpu.roll(pair_ref[i, k % 2], (LANES - 1 - k) % LANES, 1), 0.0)
        y_part = jnp.where(
            row_a, change_ref[0, i, k : k + 1, :], jnp.where(row_b, change_ref[1, i, k : k + 1, :], 0.0)
        )
        return (ref[k] + (x_part + y_part)) * inv_ref[k]

    outs = (out_t_ref, out_s_ref)
    middle = levels // 2
    zero = jnp.zeros((ROWS, LANES), jnp.float32)
    upper, lower = [zero, zero], [zero, zero]
    for j in range(middle):
        for i in range(2):
            upper[i] = right_side(i, j) + low_ref[j] * upper[i]
            outs[i][j] = upper[i]
            k = levels - 1 - j
            lower[i] = right_side(i, k) + low_ref[k] * lower[i]
            outs[i][k] = lower[i]
    for i in range(2):
        solved = right_side(i, middle) + low_ref[middle] * upper[i] + ratio_ref[middle] * lower[i]
        outs[i][middle] = solved
        upper[i] = lower[i] = solved
    for j in range(1, middle + 1):
        for i in range(2):
            k = middle - j
            upper[i] = outs[i][k] + ratio_ref[k] * upper[i]
            outs[i][k] = upper[i]
            k = middle + j
            lower[i] = outs[i][k] + ratio_ref[k] * lower[i]
            outs[i][k] = lower[i]


def call(kernel, outs, operands, memory, scratch=(), flops=0, name=None, aliases=None):
    return pl.pallas_call(
        kernel,
        out_shape=[jax.ShapeDtypeStruct(getattr(s, "shape", s), getattr(s, "dtype", jnp.float32)) for s in outs],
        in_specs=[pl.BlockSpec(memory_space=memory)] * len(operands),
        out_specs=[pl.BlockSpec(memory_space=pltpu.VMEM)] * len(outs),
        scratch_shapes=list(scratch),
        input_output_aliases=aliases or {},
        compiler_params=pltpu.CompilerParams(vmem_limit_bytes=24 * 1024 * 1024),
        cost_estimate=pl.CostEstimate(flops=flops, bytes_accessed=4 * 1024 * 1024, transcendentals=0),
        name=name,
    )(*operands)


def local(pairs, cut, heat, salt, u, v, w, kap, diff, depth):
    levels, rows, lanes = heat.shape
    block = padded(levels)
    cube, wide, thin = (levels, rows, lanes), (3 * block, lanes), (3 * rows, lanes)
    compact = (2 * block + levels // rows * rows, lanes)

    def moved(x, which):
        return lax.ppermute(x, GRID_AXES, pairs[which])

    operands = tuple(pltpu.with_memory_space_constraint(x, pltpu.HBM) for x in (heat, salt, v, u, diff, depth))
    pack_b, pack_xb, pack_xa, pack_a, own_xa, own_xb, pack_first, pack_second, heat, salt, v, u, diff, depth = call(
        functools.partial(pack_kernel, levels, cut), [wide, thin, thin, compact, thin, thin, thin, thin] + [(block, rows, lanes)] * 4 + [diff.shape, depth],
        operands, pltpu.HBM, [pltpu.SemaphoreType.DMA((6,))], name="pack",
    )
    group = next(g for g in (15, 5, 3, 2, 1) if levels % g == 0)
    operands = (heat, salt, u, v, w, kap, diff, depth, own_xa, own_xb)
    results = [cube] * 5 + [(7 * block, lanes)] * 2 + [(9 * rows, lanes)] * 2
    early = list(
        call(functools.partial(early_kernel, levels, group, cut), results, operands, pltpu.VMEM, name="early")
    )
    got_first = moved(pack_first, "first")
    pack_b, early[0] = lax.optimization_barrier((pack_b, early[0]))
    got_b = moved(pack_b, "b")
    relayed = moved(pack_xb, "relay")
    got_xb = moved(pack_second, "xb")
    got_xa = moved(pack_xa, "xa")
    got_a = moved(pack_a, "a")
    got_first, early[0] = lax.optimization_barrier((got_first, early[0]))
    star_t, star_s, inv, low, ratio, own_a, own_b, side_xa, side_xb = call(
        functools.partial(late_kernel, levels, group, cut), results, operands + tuple(early), pltpu.VMEM,
        flops=1_145_000_000, name="late", aliases={10 + i: i for i in range(9)},
    )
    relayed, star_t = lax.optimization_barrier((relayed, star_t))
    got_relay = moved(relayed, "hand_on")
    pair = call(
        functools.partial(columns_kernel, levels, cut), [(2, 2, rows, lanes)],
        (got_first, got_relay, got_xb, got_xa, side_xa, side_xb), pltpu.VMEM, name="columns",
    )[0]
    operands = (
        got_b, got_a, own_a, own_b, pair,
        star_t, star_s, inv, low, ratio,
    )
    return call(
        functools.partial(final_kernel, levels),
        [cube] * 2, operands, pltpu.VMEM, [pltpu.VMEM((2, 2, block, lanes), jnp.float32)], name="final",
    )


def is_far_row(y):
    ny = lax.axis_size("gy")
    return (y == ny // 2 - 1) | (y == ny // 2) | (y == ny - 1)


def is_far_column(x, cut):
    return (x % cut == 0) | (x % cut == cut - 1)


def solution(mesh):
    ny, nx = mesh.shape["gy"], mesh.shape["gx"]
    cut = nx // 4
    far_rows = (ny // 2 - 1, ny // 2, ny - 1)
    far_columns = [x for x in range(nx) if x % cut in (0, cut - 1)]

    def at(y, x):
        return y * nx + x

    def beside(x):
        return (((x + 1) ^ 1) - 1) % nx

    second = [(y, ((y + 1) ^ 1) - 1, x, x) for y in range(1, ny - 1) for x in range(nx)]
    second += [(ny - 1, ny - 1, x, nx - 1 - x) for x in range(nx)]
    corners = [(y, x) for y in far_rows for x in far_columns]
    pairs = {
        "a": [(at(y, x), at(y ^ 1, x)) for y in range(ny) for x in range(nx)],
        "b": [(at(y, x), at(to_y, to_x)) for y, to_y, x, to_x in second],
        "first": [(at(y, x), at(y, x ^ 1)) for y in range(ny // 2 - 1) for x in range(nx) if x % cut < cut // 2]
        + [(at(y, x), at(y, beside(x))) for y in (ny // 2 - 1,) for x in range(nx) if x % cut in (1, 2, cut - 1)],
        "xa": [(at(y, x), at(y, x ^ 1)) for y in range(ny) for x in range(nx) if y >= ny // 2 or x % cut >= (cut // 2 if y < ny // 2 - 1 else 2)],
        "xb": [(at(y, x), at(y, beside(x))) for y in range(ny) for x in range(nx) if (y, x) not in corners and (y != ny // 2 - 1 or x % cut > 2)]
        + [(at(ny // 2 - 1, x), at(ny // 2 - 1, x ^ 1)) for x in range(nx) if x % cut < 2],
        "relay": [(at(y, x), at(y ^ 1, beside(x))) for y, x in corners if y >= ny // 2 or x % cut == 0],
        "hand_on": [(at(y ^ 1, x), at(y, x)) for y, x in corners if y >= ny // 2 or x % cut == cut - 1],
    }
    cube = P(None, "gy", "gx")
    sheet = P("gy", "gx")
    return jax.shard_map(
        functools.partial(local, pairs, cut),
        mesh=mesh,
        in_specs=(cube,) * 6 + (sheet, sheet),
        out_specs=(cube, cube),
        check_vma=False,
    )
```

```python
import functools

import jax
import jax.numpy as jnp
from jax import lax
from jax.experimental import pallas as pl
from jax.experimental.pallas import tpu as pltpu
from jax.sharding import PartitionSpec as P

thermal_coef = 0.1655
haline_coef = 0.76554
thermal_curve = 0.05952
haline_curve = 0.00054914
thermal_press = 0.0001497
haline_press = 1.109e-05
cabbeling = 0.0024341
bottom_depth = 5800.0
slope_limit = 1.0
strat_offset = 0.1

ROWS = 8
LANES = 128
GRID_AXES = ("gy", "gx")


def padded(levels):
    return -(-(levels + 2) // 8) * 8


def density(temper, saline, strata_height):
    heat_slope = -thermal_coef * (1.0 + thermal_press * strata_height)
    salt_slope = haline_coef * (1.0 - haline_press * strata_height)
    return (
        heat_slope - (0.5 * thermal_coef * thermal_curve) * temper - cabbeling * saline
    ) * temper + (salt_slope - (0.5 * haline_coef * haline_curve) * saline) * saline


def quotient(top, bottom):
    return top / bottom


def face_flux(speed, half_diffus, wet, left, right):
    steps = jnp.maximum(left[5] + right[5], 0.0) + 4.0 * strat_offset
    quarter = jnp.clip(quotient(right[2] - left[2], steps), -0.25 * slope_limit, 0.25 * slope_limit)
    forward = speed > 0.0

    def one(i):
        carried = speed * jnp.where(forward, left[i], right[i])
        mixed = half_diffus * (right[i] - left[i] - quarter * (left[3 + i] + right[3 + i]))
        return jnp.where(wet, carried - mixed, 0.0)

    return one(0), one(1)


def fetch(sources, targets, sems):
    copies = [pltpu.make_async_copy(a, b, sems.at[i]) for i, (a, b) in enumerate(zip(sources, targets))]
    for copy in copies:
        copy.start()
    return copies


def pack_kernel(
    levels, cut, t_hbm, s_hbm, v_hbm, u_hbm, diff_hbm, depth_hbm,
    b_ref, xb_ref, xa_ref, a_ref, own_xa_ref, own_xb_ref, first_ref, second_ref, t_ref, s_ref, v_ref, u_ref, diff_ref, depth_ref, sems,
):
    copies = fetch(
        (t_hbm, s_hbm, v_hbm, u_hbm, diff_hbm, depth_hbm),
        [ref.at[pl.ds(0, levels)] for ref in (t_ref, s_ref, v_ref, u_ref)] + [diff_ref, depth_ref],
        sems,
    )
    block = padded(levels)
    gy, gx = lax.axis_index("gy"), lax.axis_index("gx")
    y_even, x_even = gy % 2 == 0, gx % 2 == 0
    is_top = gy == lax.axis_size("gy") - 1
    lane = lax.broadcasted_iota(jnp.int32, (block, LANES), 1)
    source = jnp.where(is_top, LANES - 1 - lane, lane)
    one_lane = lax.broadcasted_iota(jnp.int32, (ROWS, LANES), 1)
    copies[4].wait()
    copies[5].wait()
    depth = depth_ref[...].astype(jnp.float32)
    diff = diff_ref[...]
    for ref in (t_ref, s_ref, v_ref, u_ref):
        ref[levels:] = jnp.zeros((block - levels, ROWS, LANES), jnp.float32)
    index = lax.broadcasted_iota(jnp.int32, (block, LANES), 0)

    def row_part(ref, i):
        ref = ref.reshape(block * ROWS, LANES)
        top = ref[pl.ds(ROWS - 1, block, stride=ROWS), :]
        low = ref[pl.ds(0, block, stride=ROWS), :]
        near, far = jnp.where(y_even, top, low), jnp.where(y_even, low, top)
        if i == 0:
            for name, value in ((levels, diff), (levels + 1, depth)):
                near = jnp.where(index == name, jnp.where(y_even, value[ROWS - 1 :], value[:1]), near)
                far = jnp.where(index == name, jnp.where(y_even, value[:1], value[ROWS - 1 :]), far)
        b_ref[i * block : (i + 1) * block] = jnp.take_along_axis(far, source, axis=1, mode="promise_in_bounds")
        if i < 2:
            a_ref[i * block : (i + 1) * block] = near
        else:
            whole = levels // ROWS * ROWS
            a_ref[2 * block :] = near[:whole]
            a_ref[block - (levels - whole) : block] = near[whole:levels]

    def column_part(ref, i):
        planes = [ref[k] for k in range(levels)]
        if i == 0:
            planes += [diff, depth]
        zero = jnp.zeros((ROWS, LANES), jnp.float32)
        east, west = [zero] * 8, [zero] * 8
        for k, plane in enumerate(planes):
            moved = pltpu.roll(plane, k + 1, 1)
            east[k % 8] = jnp.where(one_lane == k, moved, east[k % 8])
            if i < 2:
                west[k % 8] = jnp.where(one_lane == k + 1, moved, west[k % 8])
        east = functools.reduce(jnp.add, east)
        west = functools.reduce(jnp.add, west)
        part = slice(i * ROWS, (i + 1) * ROWS)
        own_xa_ref[part] = jnp.where(x_even, east, west)
        own_xb_ref[part] = jnp.where(x_even, west, east)
        east, west = pltpu.roll(east, 1, 1), pltpu.roll(west, LANES - 1, 1)
        xa, xb = jnp.where(x_even, east, west), jnp.where(x_even, west, east)
        xa_ref[part] = xa
        xb_ref[part] = xb
        first_ref[part] = jnp.where(below_middle(gy), xb, xa)
        second_ref[part] = jnp.where(jnp.logical_and(below_middle(gy), gx % cut < 2), xa, xb)

    copies[0].wait()
    copies[1].wait()
    for i, ref in enumerate((t_ref, s_ref)):
        row_part(ref, i)
        column_part(ref, i)
    copies[2].wait()
    copies[3].wait()
    row_part(v_ref, 2)
    column_part(u_ref, 2)


def below_middle(gy):
    return gy == lax.axis_size("gy") // 2 - 1


def starts_early(gy, gx, cut):
    ny = lax.axis_size("gy")
    return jnp.logical_and(gy < ny // 2, gx % cut < cut // 2)


def early_kernel(levels, group, cut, *refs):
    @pl.when(starts_early(lax.axis_index("gy"), lax.axis_index("gx"), cut))
    def _():
        inner(levels, group, *refs)


def late_kernel(levels, group, cut, *refs):
    n_in, n_out = 10, 9
    ins, outs = refs[:n_in], refs[n_in + n_out :]

    @pl.when(jnp.logical_not(starts_early(lax.axis_index("gy"), lax.axis_index("gx"), cut)))
    def _():
        inner(levels, group, *ins, *outs)


def inner(
    levels, group, t_ref, s_ref, u_ref, v_ref, w_ref, kap_ref, diff_ref, depth_ref,
    own_xa_ref, own_xb_ref, star_t_ref, star_s_ref, inv_ref, low_ref, ratio_ref, own_a_ref, own_b_ref,
    side_xa_ref, side_xb_ref,
):
    block = padded(levels)
    depth = depth_ref[...]
    diff = diff_ref[...]
    lane = lax.broadcasted_iota(jnp.int32, (ROWS, LANES), 1)
    row = lax.broadcasted_iota(jnp.int32, (ROWS, LANES), 0)

    def east(x):
        return pltpu.roll(x, LANES - 1, 1)

    def west(x):
        return pltpu.roll(x, 1, 1)

    def north(x):
        return pltpu.roll(x, ROWS - 1, 0)

    def south(x):
        return pltpu.roll(x, 1, 0)

    depth_x = jnp.where(lane == LANES - 1, 0, jnp.minimum(depth, east(depth)))
    depth_y = jnp.where(row == ROWS - 1, 0, jnp.minimum(depth, north(depth)))
    diff_x = 0.5 * (diff + east(diff))
    diff_y = 0.5 * (diff + north(diff))

    def at(ref, k):
        return ref[k]

    def height(k):
        part = (k.astype(jnp.float32) + 0.5) / levels
        return bottom_depth * (part * part)

    def level(k, carry):
        t, s, dens, step_t, step_s, step_d, top_t, top_s = carry
        below = jnp.minimum(k + 1, levels - 1)
        open_below = k + 1 < depth
        t1, s1 = at(t_ref, below), at(s_ref, below)
        dens1 = density(t1, s1, height(below))
        next_t = jnp.where(open_below, t1 - t, 0.0)
        next_s = jnp.where(open_below, s1 - s, 0.0)
        next_d = jnp.where(open_below, dens1 - dens, 0.0)
        w1 = at(w_ref, below)
        up = w1 > 0.0
        low_t = jnp.where(open_below, w1 * jnp.where(up, t1, t), 0.0)
        low_s = jnp.where(open_below, w1 * jnp.where(up, s1, s), 0.0)
        here = (t, s, dens, step_t + next_t, step_s + next_s, step_d + next_d)
        fx_t, fx_s = face_flux(at(u_ref, k), diff_x, k < depth_x, here, tuple(map(east, here)))
        fy_t, fy_s = face_flux(at(v_ref, k), diff_y, k < depth_y, here, tuple(map(north, here)))
        star_t_ref[k] = t - (fx_t - west(fx_t)) - (fy_t - south(fy_t)) - (top_t - low_t)
        star_s_ref[k] = s - (fx_s - west(fx_s)) - (fy_s - south(fy_s)) - (top_s - low_s)
        return t1, s1, dens1, next_t, next_s, next_d, low_t, low_s

    zero = jnp.zeros((ROWS, LANES), jnp.float32)
    t0, s0 = t_ref[0], s_ref[0]
    first = (t0, s0, density(t0, s0, bottom_depth * (0.5 / levels) ** 2), zero, zero, zero, zero, zero)

    middle = levels // 2

    def coupling(k):
        return jnp.where(k < depth, kap_ref[k], 0.0)

    def eliminate(j, carry):
        above, ratio, below, ratio_up = carry
        k = j
        under = coupling(k + 1)
        inv = quotient(1.0, 1.0 + above + under - above * ratio)
        inv_ref[k] = inv
        low_ref[k] = above * inv
        ratio = under * inv
        ratio_ref[k] = ratio
        k = levels - 1 - j
        over = coupling(k)
        inv = quotient(1.0, 1.0 + over + below - below * ratio_up)
        inv_ref[k] = inv
        low_ref[k] = below * inv
        ratio_up = over * inv
        ratio_ref[k] = ratio_up
        return under, ratio, over, ratio_up

    rounds = levels // group
    pairs = min((middle // rounds, -(-middle // rounds)), key=lambda p: middle - min(rounds, middle // p) * p)
    whole = min(rounds, middle // pairs)

    def both(i, carry):
        one, two = carry
        for j in range(group):
            one = level(i * group + j, one)
            if j < pairs:
                two = eliminate(i * pairs + j, two)
        return one, two

    def some(i, carry):
        for j in range(group):
            carry = level(i * group + j, carry)
        return carry

    carry, elimination = lax.fori_loop(0, whole, both, (first, (zero, zero, zero, zero)))
    lax.fori_loop(whole, rounds, some, carry)
    for j in range(whole * pairs, middle):
        elimination = eliminate(jnp.int32(j), elimination)
    above, ratio, below, ratio_up = elimination
    inv = 1.0 / (1.0 + above + below - above * ratio - below * ratio_up)
    inv_ref[middle] = inv
    low_ref[middle] = above * inv
    ratio_ref[middle] = below * inv

    gy = lax.axis_index("gy")
    y_even = gy % 2 == 0
    depth_f = depth.astype(jnp.float32)
    index = lax.broadcasted_iota(jnp.int32, (block, LANES), 0)
    heights = level_heights(index, levels)
    flats = [ref.reshape(block * ROWS, LANES) for ref in (t_ref, s_ref, v_ref)]
    tops = [flat[pl.ds(ROWS - 1, block, stride=ROWS), :] for flat in flats]
    lows = [flat[pl.ds(0, block, stride=ROWS), :] for flat in flats]
    for own_ref, keep_top in ((own_a_ref, y_even), (own_b_ref, jnp.logical_not(y_even))):
        t, s, q = (jnp.where(keep_top, top, low) for top, low in zip(tops, lows))
        edge_diff, edge_depth = (
            jnp.where(keep_top, value[ROWS - 1 :], value[:1]) for value in (diff, depth_f)
        )
        for i, field in enumerate(side(t, s, edge_depth, index.astype(jnp.float32), heights, 0) + (q,)):
            if i == 0:
                field = jnp.where(index == levels, edge_diff, jnp.where(index == levels + 1, edge_depth, field))
            own_ref[i * block : (i + 1) * block] = field
    x_even = lax.axis_index("gx") % 2 == 0
    for own_ref, side_ref, own_left in ((own_xa_ref, side_xa_ref, x_even), (own_xb_ref, side_xb_ref, jnp.logical_not(x_even))):
        t, s, q = (own_ref[i * ROWS : (i + 1) * ROWS] for i in range(3))
        ahead = jnp.where(own_left, 0, 1)
        values = column_side(t, s, levels, ahead) + (q,) + edge_values(t, levels, ahead)
        for i, value in enumerate(values):
            side_ref[i * ROWS : (i + 1) * ROWS] = value


def level_heights(index, levels):
    part = (index.astype(jnp.float32) + 0.5) / levels
    return bottom_depth * (part * part)


def column_sums(x, open_here, axis):
    size = x.shape[axis]
    step = jnp.where(open_here, x - pltpu.roll(x, 1, axis), 0.0)
    return step + pltpu.roll(step, size - 1, axis)


def side(temper, saline, depth, index, heights, axis):
    dens = density(temper, saline, heights)
    open_here = jnp.logical_and(index >= 1, index < depth)
    return (
        temper,
        saline,
        dens,
        column_sums(temper, open_here, axis),
        column_sums(saline, open_here, axis),
        column_sums(dens, open_here, axis),
    )


def edge_values(t, levels, ahead):
    one, two, three = (t[:, levels + i : levels + i + 1] for i in range(3))
    first, second = jnp.where(ahead == 0, one, two), jnp.where(ahead == 0, two, three)
    return jnp.broadcast_to(first, t.shape), jnp.broadcast_to(second, t.shape)


def column_side(t, s, levels, ahead):
    depth = edge_values(t, levels, ahead)[1]
    level = lax.broadcasted_iota(jnp.int32, t.shape, 1) - ahead
    here, over, under = (
        (
            pltpu.roll(t, shift, 1) if shift else t,
            pltpu.roll(s, shift, 1) if shift else s,
            level_heights(level - move, levels),
        )
        for shift, move in ((0, 0), (1, 1), (LANES - 1, -1))
    )
    level = level.astype(jnp.float32)
    open_here = jnp.logical_and(level >= 1.0, level < depth)
    open_under = level + 1.0 < depth
    here, over, under = (x[:2] + (density(*x),) for x in (here, over, under))
    sums = tuple(
        jnp.where(open_here, h - o, 0.0) + jnp.where(open_under, u - h, 0.0) for h, o, u in zip(here, over, under)
    )
    return here + sums


def edge_change(own, got, own_speed, got_speed, diffus, wet, own_left, fold=None):
    sign = jnp.where(own_left, 1.0, -1.0)
    speed = jnp.where(own_left, own_speed, got_speed)
    if fold is not None:
        speed = jnp.where(fold, 0.5 * (own_speed - got_speed), speed)
    outward = sign * speed
    steps = jnp.maximum(own[5] + got[5], 0.0) + 4.0 * strat_offset
    quarter = jnp.clip(quotient(got[2] - own[2], steps), -0.25 * slope_limit, 0.25 * slope_limit)
    leaves = outward > 0.0

    def one(i):
        carried = outward * jnp.where(leaves, own[i], got[i])
        mixed = diffus * (got[i] - own[i] - quarter * (own[3 + i] + got[3 + i]))
        return jnp.where(wet, mixed - carried, 0.0)

    return one(0), one(1)


def columns_kernel(levels, cut, got_first, got_relay, got_xb, got_xa, side_xa, side_xb, pair_ref):
    gy, gx = lax.axis_index("gy"), lax.axis_index("gx")
    x_even = gx % 2 == 0
    x_odd = jnp.logical_not(x_even)
    corner = jnp.logical_and(is_far_row(gy), is_far_column(gx, cut))
    xb_first = jnp.logical_and(below_middle(gy), gx % cut < 3)
    xa_first = jnp.logical_and(starts_early(gy, gx, cut), jnp.logical_not(below_middle(gy)))

    lane = lax.broadcasted_iota(jnp.int32, (ROWS, LANES), 1)

    def column_change(side_ref, got, own_left):
        own = [side_ref[i * ROWS : (i + 1) * ROWS] for i in range(9)]
        ahead = jnp.where(own_left, 0, 1)
        diffus, depth = edge_values(got[0], levels, ahead)
        level = (lane - ahead).astype(jnp.float32)
        wet = jnp.logical_and(level >= 0.0, level < jnp.minimum(own[8], depth))
        return edge_change(
            own, column_side(got[0], got[1], levels, ahead), own[6], got[2], 0.5 * (own[7] + diffus), wet, own_left
        )

    def thirds(ref):
        return [ref[i * ROWS : (i + 1) * ROWS] for i in range(3)]

    first, relay = thirds(got_first), thirds(got_relay)
    xa_second = jnp.logical_and(below_middle(gy), gx % cut < 2)
    from_xa = [
        jnp.where(xa_first, a, jnp.where(xa_second, b, c))
        for a, b, c in zip(first, thirds(got_xb), thirds(got_xa))
    ]
    from_xb = [
        jnp.where(xb_first, a, jnp.where(corner, b, c)) for a, b, c in zip(first, relay, thirds(got_xb))
    ]
    change_xa = column_change(side_xa, from_xa, x_even)
    change_xb = column_change(side_xb, from_xb, x_odd)
    even_lane = lane % 2 == 0
    for i in range(2):
        last = jnp.where(x_even, change_xa[i], change_xb[i])
        first = jnp.where(x_even, change_xb[i], change_xa[i])
        pair_ref[i, 0] = jnp.where(even_lane, last, first)
        pair_ref[i, 1] = jnp.where(even_lane, first, last)


def final_kernel(
    levels, got_b, got_a, own_a, own_b, pair_ref,
    star_t_ref, star_s_ref, inv_ref, low_ref, ratio_ref,
    out_t_ref, out_s_ref, change_ref,
):
    block = padded(levels)
    gy = lax.axis_index("gy")
    y_even = gy % 2 == 0
    y_odd = jnp.logical_not(y_even)
    is_top = gy == lax.axis_size("gy") - 1
    index = lax.broadcasted_iota(jnp.int32, (block, LANES), 0)
    height = level_heights(index, levels)
    level = index.astype(jnp.float32)

    def row_change(place, own_ref, t, s, q, own_left, fold):
        own = [own_ref[i * block : (i + 1) * block] for i in range(7)]
        diffus, depth = t[levels : levels + 1], t[levels + 1 : levels + 2]
        own_diffus, own_depth = own[0][levels : levels + 1], own[0][levels + 1 : levels + 2]
        changes = edge_change(
            own, side(t, s, depth, level, height, 0), own[6], q,
            0.5 * (own_diffus + diffus), level < jnp.minimum(own_depth, depth), own_left, fold,
        )
        for i in range(2):
            change_ref[place, i] = changes[i]

    whole = levels // ROWS * ROWS
    t, s = got_a[:block], got_a[block : 2 * block]
    q = jnp.concatenate(
        [got_a[2 * block :], t[block - (levels - whole) :], jnp.zeros((block - levels, LANES), jnp.float32)], 0
    )
    row_change(0, own_a, t, s, q, y_even, None)
    row_change(1, own_b, *(got_b[i * block : (i + 1) * block] for i in range(3)), y_odd, is_top)

    lane = lax.broadcasted_iota(jnp.int32, (ROWS, LANES), 1)
    row = lax.broadcasted_iota(jnp.int32, (ROWS, LANES), 0)
    at_side = jnp.logical_or(lane == 0, lane == LANES - 1)
    row_a = row == jnp.where(y_even, ROWS - 1, 0)
    row_b = row == jnp.where(y_even, 0, ROWS - 1)

    def right_side(i, k):
        ref = (star_t_ref, star_s_ref)[i]
        x_part = jnp.where(at_side, pltpu.roll(pair_ref[i, k % 2], (LANES - 1 - k) % LANES, 1), 0.0)
        y_part = jnp.where(
            row_a, change_ref[0, i, k : k + 1, :], jnp.where(row_b, change_ref[1, i, k : k + 1, :], 0.0)
        )
        return (ref[k] + (x_part + y_part)) * inv_ref[k]

    outs = (out_t_ref, out_s_ref)
    middle = levels // 2
    zero = jnp.zeros((ROWS, LANES), jnp.float32)
    upper, lower = [zero, zero], [zero, zero]
    for j in range(middle):
        for i in range(2):
            upper[i] = right_side(i, j) + low_ref[j] * upper[i]
            outs[i][j] = upper[i]
            k = levels - 1 - j
            lower[i] = right_side(i, k) + low_ref[k] * lower[i]
            outs[i][k] = lower[i]
    for i in range(2):
        solved = right_side(i, middle) + low_ref[middle] * upper[i] + ratio_ref[middle] * lower[i]
        outs[i][middle] = solved
        upper[i] = lower[i] = solved
    for j in range(1, middle + 1):
        for i in range(2):
            k = middle - j
            upper[i] = outs[i][k] + ratio_ref[k] * upper[i]
            outs[i][k] = upper[i]
            k = middle + j
            lower[i] = outs[i][k] + ratio_ref[k] * lower[i]
            outs[i][k] = lower[i]


def call(kernel, outs, operands, memory, scratch=(), flops=0, name=None, aliases=None):
    return pl.pallas_call(
        kernel,
        out_shape=[jax.ShapeDtypeStruct(getattr(s, "shape", s), getattr(s, "dtype", jnp.float32)) for s in outs],
        in_specs=[pl.BlockSpec(memory_space=memory)] * len(operands),
        out_specs=[pl.BlockSpec(memory_space=pltpu.VMEM)] * len(outs),
        scratch_shapes=list(scratch),
        input_output_aliases=aliases or {},
        compiler_params=pltpu.CompilerParams(vmem_limit_bytes=24 * 1024 * 1024),
        cost_estimate=pl.CostEstimate(flops=flops, bytes_accessed=4 * 1024 * 1024, transcendentals=0),
        name=name,
    )(*operands)


def local(pairs, cut, heat, salt, u, v, w, kap, diff, depth):
    levels, rows, lanes = heat.shape
    block = padded(levels)
    cube, wide, thin = (levels, rows, lanes), (3 * block, lanes), (3 * rows, lanes)
    compact = (2 * block + levels // rows * rows, lanes)

    def moved(x, which):
        return lax.ppermute(x, GRID_AXES, pairs[which])

    operands = tuple(pltpu.with_memory_space_constraint(x, pltpu.HBM) for x in (heat, salt, v, u, diff, depth))
    pack_b, pack_xb, pack_xa, pack_a, own_xa, own_xb, pack_first, pack_second, heat, salt, v, u, diff, depth = call(
        functools.partial(pack_kernel, levels, cut), [wide, thin, thin, compact, thin, thin, thin, thin] + [(block, rows, lanes)] * 4 + [diff.shape, depth],
        operands, pltpu.HBM, [pltpu.SemaphoreType.DMA((6,))], name="pack",
    )
    group = next(g for g in (15, 5, 3, 2, 1) if levels % g == 0)
    operands = (heat, salt, u, v, w, kap, diff, depth, own_xa, own_xb)
    results = [cube] * 5 + [(7 * block, lanes)] * 2 + [(9 * rows, lanes)] * 2
    early = list(
        call(functools.partial(early_kernel, levels, group, cut), results, operands, pltpu.VMEM, name="early")
    )
    got_first = moved(pack_first, "first")
    pack_b, early[0] = lax.optimization_barrier((pack_b, early[0]))
    got_b = moved(pack_b, "b")
    relayed = moved(pack_xb, "relay")
    got_xb = moved(pack_second, "xb")
    got_xa = moved(pack_xa, "xa")
    got_a = moved(pack_a, "a")
    got_first, early[0] = lax.optimization_barrier((got_first, early[0]))
    star_t, star_s, inv, low, ratio, own_a, own_b, side_xa, side_xb = call(
        functools.partial(late_kernel, levels, group, cut), results, operands + tuple(early), pltpu.VMEM,
        flops=1_145_000_000, name="late", aliases={10 + i: i for i in range(9)},
    )
    relayed, star_t = lax.optimization_barrier((relayed, star_t))
    got_relay = moved(relayed, "hand_on")
    pair = call(
        functools.partial(columns_kernel, levels, cut), [(2, 2, rows, lanes)],
        (got_first, got_relay, got_xb, got_xa, side_xa, side_xb), pltpu.VMEM, name="columns",
    )[0]
    operands = (
        got_b, got_a, own_a, own_b, pair,
        star_t, star_s, inv, low, ratio,
    )
    return call(
        functools.partial(final_kernel, levels),
        [cube] * 2, operands, pltpu.VMEM, [pltpu.VMEM((2, 2, block, lanes), jnp.float32)], name="final",
    )


def is_far_row(y):
    ny = lax.axis_size("gy")
    return (y == ny // 2 - 1) | (y == ny // 2) | (y == ny - 1)


def is_far_column(x, cut):
    return (x % cut == 0) | (x % cut == cut - 1)


def solution(mesh):
    ny, nx = mesh.shape["gy"], mesh.shape["gx"]
    cut = nx // 4
    far_rows = (ny // 2 - 1, ny // 2, ny - 1)
    far_columns = [x for x in range(nx) if x % cut in (0, cut - 1)]

    def at(y, x):
        return y * nx + x

    def beside(x):
        return (((x + 1) ^ 1) - 1) % nx

    second = [(y, ((y + 1) ^ 1) - 1, x, x) for y in range(1, ny - 1) for x in range(nx)]
    second += [(ny - 1, ny - 1, x, nx - 1 - x) for x in range(nx)]
    corners = [(y, x) for y in far_rows for x in far_columns]
    pairs = {
        "a": [(at(y, x), at(y ^ 1, x)) for y in range(ny) for x in range(nx)],
        "b": [(at(y, x), at(to_y, to_x)) for y, to_y, x, to_x in second],
        "first": [(at(y, x), at(y, x ^ 1)) for y in range(ny // 2 - 1) for x in range(nx) if x % cut < cut // 2]
        + [(at(y, x), at(y, beside(x))) for y in (ny // 2 - 1,) for x in range(nx) if x % cut in (1, 2, cut - 1)],
        "xa": [(at(y, x), at(y, x ^ 1)) for y in range(ny) for x in range(nx) if y >= ny // 2 or x % cut >= (cut // 2 if y < ny // 2 - 1 else 2)],
        "xb": [(at(y, x), at(y, beside(x))) for y in range(ny) for x in range(nx) if (y, x) not in corners and (y != ny // 2 - 1 or x % cut > 2)]
        + [(at(ny // 2 - 1, x), at(ny // 2 - 1, x ^ 1)) for x in range(nx) if x % cut < 2],
        "relay": [(at(y, x), at(y ^ 1, beside(x))) for y, x in corners if y >= ny // 2 or x % cut == 0],
        "hand_on": [(at(y ^ 1, x), at(y, x)) for y, x in corners if y >= ny // 2 or x % cut == cut - 1],
    }
    cube = P(None, "gy", "gx")
    sheet = P("gy", "gx")
    return jax.shard_map(
        functools.partial(local, pairs, cut),
        mesh=mesh,
        in_specs=(cube,) * 6 + (sheet, sheet),
        out_specs=(cube, cube),
        check_vma=False,
    )
```
